32 devices in a mesh: section: 4 (over y, core), row: 8 (over z, x).
Axes of the slice: x: 2, y: 2, z: 4, core: 2. Of those that a mesh axis runs over, the one named last changes fastest.
Arguments:
- coupling: bfloat16 [512, 128, 128], P(('section', 'row')), may hold values from -4 to 4
- diag_inverse: float32 [512, 128, 128], P(('section', 'row')), may hold values from -0.046875 to 0.046875
- pivot_inverse: bfloat16 [128, 128, 128], P(('section', 'row')), may hold values from -0.5 to 0.5
- cross_left: bfloat16 [4096, 128, 128], P(('section', 'row')), may hold values from -0.5 to 0.5
- cross_right: bfloat16 [4096, 128, 128], P(('section', 'row')), may hold values from -4 to 4
- cross_pivot: int32 [4096], P(('section', 'row')), may hold values from 0 to 3
- cross_owner: int32 [4096, 1], P(('section', 'row')), may hold values from 0 to 7; in each aligned block of 128 rows (0 to 127, 128 to 255, ...) at most 16 rows name the same one
- foreign_target_row: int32 [4096], P(('section', 'row')), may hold values from 0 to 15
- cross_count: int32 [32], P(('section', 'row')), may hold values from 1 to 128, 3072 in all
- local_left: bfloat16 [4096, 128, 128], P(('section', 'row')), may hold values from -0.5 to 0.5
- local_right: bfloat16 [4096, 128, 128], P(('section', 'row')), may hold values from -4 to 4
- local_pivot: int32 [4096], P(('section', 'row')), may hold values from 0 to 3
- local_target: int32 [4096], P(('section', 'row')), may hold values from 0 to 15
- adjoint_seed: float32 [512, 128, 128], P(('section', 'row')), may hold values from -48 to 48
Outputs:
- coupling_new: float32 [512, 128, 128], P(('section', 'row'))
- adjoint: float32 [512, 128, 128], P(('section', 'row'))
The draws below stay inside these ranges and needn't reach their ends.
Inputs may be any that keep to these rules, and one draw needn't show every extreme that they name: `cross_owner`: among the 128 cross slots of one device, live or not, at most 16 name the same owner, a bound that some block reaches of them. `cross_count`: some device has all its cross slots live.
All inputs are finite; a program needn't handle non-finite values.
Results may differ from the reference program's by a relative error of at most 0.0089.
Values may be sent and summed in bfloat16 or wider, within the bound.
A program may use at most 192 MiB of HBM per device.

```python
import math
import jax
import jax.numpy as jnp
import numpy as np
from jax import lax

B = 128
ROWS_DEV = 16
UPD_DEV = 128
LOC_DEV = 128
PIV_DEV = 4
NRHS = 128
NBLK = 512
SLOTS = 4096
LSLOTS = 4096
PIVOTS = 128
N_SECTION = 4
N_ROW = 8


def with_ends(result, key, low, top_value):
    spot = [jax.random.randint(jax.random.fold_in(key, axis), (), 0, length) for axis, length in enumerate(result.shape)]
    widest = result.shape.index(max(result.shape))
    beside = spot[:widest] + [(spot[widest] + 1) % result.shape[widest]] + spot[widest + 1:]
    return result.at[tuple(spot)].set(low).at[tuple(beside)].set(top_value)


def steps_of(key, dims, split, low, high):
    def one(position, shards_of):
        draws = jax.random.uniform(jax.random.fold_in(jax.random.fold_in(key, 6), position), (shards_of,), jnp.float32, low / len(split), high / len(split))
        return jnp.repeat(jnp.exp(draws), dims[position] // shards_of).reshape((-1,) + (1,) * (len(dims) - position - 1))

    gain = one(*split[0])
    for cut in split[1:]:
        gain = gain * one(*cut)
    return gain


def length_profile(number_of, total, limit, slope):
    portions = [(1 << 20) // math.isqrt(standing ** slope) + 1 for standing in range(2, number_of + 1)]
    spare, given = total - limit - (number_of - 1), [1] * (number_of - 1)
    while spare > 0:
        free = [i for i in range(number_of - 1) if given[i] < limit]
        pool, left = sum([portions[i] for i in free]), spare
        for i in free:
            extra = min(limit - given[i], max(1, left * portions[i] // pool), spare)
            given[i] = given[i] + extra
            spare = spare - extra
    return np.array([limit] + given)


def ragged_sizes(stream_key, count, total, bound, slope):
    if count == 2:
        one = jax.random.randint(stream_key, (), max(1, total - bound), min(bound, total - 1) + 1)
        return jnp.stack([one, total - one])
    lengths = jnp.asarray(length_profile(count, total, bound, slope), jnp.int32)
    pairs = (count - 1) // 2
    donor, receiver = lengths[1:1 + 2 * pairs:2], lengths[2:2 + 2 * pairs:2]
    room = jnp.minimum(donor - 1, bound - receiver)
    moved = jax.random.randint(jax.random.fold_in(stream_key, 1), (pairs,), 0, 1 << 20) % (room + 1)
    lengths = lengths.at[1:1 + 2 * pairs:2].set(donor - moved).at[2:2 + 2 * pairs:2].set(receiver + moved)
    return lengths[jax.random.permutation(jax.random.fold_in(stream_key, 2), count)]


def deal_out(rng, own, number, rows, count, top, reach, slope):
    order = jax.random.permutation(rng, count)
    crowded, ordinary = load_shares(count, rows * top, reach, slope, True), load_shares(count, rows * top, reach, slope, False)
    places = jnp.arange(count)

    def named(tallies, offset_by):
        used = int((tallies > 0).sum())
        fixed = max(1, used // 4)
        moved = fixed + (places - fixed + offset_by * (used - fixed)) % max(1, count - fixed)
        return jnp.zeros((count,), jnp.int32).at[order[jnp.where(places < fixed, places, moved)]].set(jnp.asarray(tallies, jnp.int32))

    tallies = jnp.where(number % 4 == 0, named(crowded, number // 4), named(ordinary, number - number // 4 - 1))
    mixed = jax.random.permutation(jax.random.fold_in(own, 3), count)
    giver, taker = mixed[0:count // 2 * 2:2], mixed[1:count // 2 * 2:2]
    margin = jnp.minimum(tallies[giver] - 1, reach - tallies[taker]) // 2
    margin = jnp.where((giver == order[0]) | (taker == order[0]) | (tallies[taker] == 0), 0, jnp.maximum(margin, 0))
    moved = jax.random.randint(jax.random.fold_in(own, 4), (count // 2,), 0, 1 << 20) % (margin + 1)
    tallies = tallies.at[giver].add(-moved).at[taker].add(moved)
    members = jnp.searchsorted(jnp.cumsum(tallies), jnp.arange(rows * top), side="right").astype(jnp.int32)
    grid = members.reshape(top, rows).T
    grid = grid[jax.random.permutation(jax.random.fold_in(own, 1), rows)]
    offset_by = jax.random.randint(jax.random.fold_in(own, 2), (rows, 1), 0, top)
    return jnp.take_along_axis(grid, (jnp.arange(top)[None, :] + offset_by) % top, axis=1)


def load_shares(count, total, limit, slope, full):
    loads = [(1 << 20) // math.isqrt(grade ** slope) + 1 for grade in range(1, count + 1)]
    largest = limit if full else min(limit, max(-(-total // count), total * loads[0] // sum(loads)))
    least = 1 if total - largest >= count - 1 else 0
    counts, rest = [largest] + [least] * (count - 1), total - largest - least * (count - 1)
    while rest > 0:
        free = [i for i in range(1, count) if counts[i] < largest] or [i for i in range(1, count) if counts[i] < limit]
        mass, left = sum([loads[i] for i in free]), rest
        for i in free:
            extra = min(limit - counts[i], max(1, left * loads[i] // mass), rest)
            counts[i] = counts[i] + extra
            rest = rest - extra
    return np.array(counts)


def gaussian(key, extent, spread, reach, shards=(), held_as=jnp.bfloat16):
    array = jax.random.normal(key, extent, jnp.float32) * spread
    if len(shards) > 0:
        array = steps_of(key, extent, shards, -0.22, 0.18) * array
    return jnp.clip(array, min=-reach, max=reach).astype(held_as)


def setup_inputs(seed: int = 0) -> dict:
    seeds = jax.random.split(jax.random.key(seed), 15)
    coupling = gaussian(seeds[0], (NBLK, B, B), 0.3, 4.0, ((0, 32),))
    diag_inverse = gaussian(seeds[1], (NBLK, B, B), (B * B) ** -0.5, 0.046875, ((0, 32),), jnp.float32)
    pivot_inverse = gaussian(seeds[2], (PIVOTS, B, B), B ** -0.5, 0.5, ((0, 32),))
    cross_left = gaussian(seeds[3], (SLOTS, B, B), B ** -0.5, 0.5, ((0, 32),))
    cross_right = gaussian(seeds[4], (SLOTS, B, B), 0.25, 4.0, ((0, 32),))
    cross_pivot = with_ends(jax.random.randint(seeds[5], (SLOTS,), 0, PIV_DEV), jax.random.fold_in(seeds[5], 1), 0, PIV_DEV - 1).astype(jnp.int32)
    cross_owner_keys = jax.random.split(jax.random.fold_in(seeds[6], 1), SLOTS // UPD_DEV)
    cross_owner_turns = jax.random.permutation(jax.random.fold_in(seeds[6], 3), SLOTS // UPD_DEV)
    cross_owner = jax.vmap(lambda own, number: deal_out(jax.random.fold_in(seeds[6], 2), own, number, UPD_DEV, N_ROW, 1, UPD_DEV // 8, 2))(cross_owner_keys, cross_owner_turns).reshape((SLOTS, 1))
    foreign_target_row = with_ends(jax.random.randint(seeds[7], (SLOTS,), 0, ROWS_DEV), jax.random.fold_in(seeds[7], 1), 0, ROWS_DEV - 1).astype(jnp.int32)
    cross_count = ragged_sizes(seeds[8], N_SECTION * N_ROW, N_SECTION * N_ROW * UPD_DEV * 3 // 4, UPD_DEV, 2).astype(jnp.int32)
    local_left = gaussian(seeds[9], (LSLOTS, B, B), B ** -0.5, 0.5, ((0, 32),))
    local_right = gaussian(seeds[10], (LSLOTS, B, B), 0.25, 4.0, ((0, 32),))
    local_pivot = with_ends(jax.random.randint(seeds[11], (LSLOTS,), 0, PIV_DEV), jax.random.fold_in(seeds[11], 1), 0, PIV_DEV - 1).astype(jnp.int32)
    local_target = with_ends(jax.random.randint(seeds[12], (LSLOTS,), 0, ROWS_DEV), jax.random.fold_in(seeds[12], 1), 0, ROWS_DEV - 1).astype(jnp.int32)
    adjoint_seed = gaussian(seeds[13], (NBLK, NRHS, B), (B // 16), 48.0, ((0, 32),), jnp.float32)
    return dict(coupling=coupling, diag_inverse=diag_inverse, pivot_inverse=pivot_inverse, cross_left=cross_left, cross_right=cross_right, cross_pivot=cross_pivot, cross_owner=cross_owner, foreign_target_row=foreign_target_row, cross_count=cross_count, local_left=local_left, local_right=local_right, local_pivot=local_pivot, local_target=local_target, adjoint_seed=adjoint_seed)


precise = lax.Precision.HIGHEST


def scaled_products(lower_factor_blocks, upper_factor_blocks, selected_entry):
    rescaled_blocks = jnp.einsum("zmq,zqy->zmy", lower_factor_blocks.astype(jnp.float32), selected_entry.astype(jnp.float32)).astype(jnp.bfloat16)
    return jnp.einsum("zmq,zqy->zmy", rescaled_blocks.astype(jnp.float32), upper_factor_blocks.astype(jnp.float32)).astype(jnp.bfloat16)


def reference(coupling, diag_inverse, pivot_inverse, cross_left, cross_right, cross_pivot, cross_owner, foreign_target_row, cross_count, local_left, local_right, local_pivot, local_target, adjoint_seed):
    devices = N_SECTION * N_ROW
    total_rows = ROWS_DEV * devices
    width = coupling.shape[1]
    pivot_table = pivot_inverse.reshape(devices, PIV_DEV, width, width)
    inputs = (
        jnp.arange(devices, dtype=jnp.int32),
        cross_left.reshape(devices, UPD_DEV, width, width),
        cross_right.reshape(devices, UPD_DEV, width, width),
        cross_pivot.reshape(devices, UPD_DEV),
        cross_owner.reshape(devices, UPD_DEV),
        foreign_target_row.reshape(devices, UPD_DEV),
        cross_count,
        local_left.reshape(devices, LOC_DEV, width, width),
        local_right.reshape(devices, LOC_DEV, width, width),
        local_pivot.reshape(devices, LOC_DEV),
        local_target.reshape(devices, LOC_DEV),
        pivot_table,
    )

    def per_device(updated, pieces):
        (device, portion_lower_factor, piece_right, piece_pivot, piece_owner, piece_target, piece_count,
         own_left, own_right, own_pivot, own_target, piece_table) = pieces
        cross_blocks = scaled_products(portion_lower_factor, piece_right, piece_table[piece_pivot])
        local_blocks = scaled_products(own_left, own_right, piece_table[own_pivot])
        section_first = (device // N_ROW) * N_ROW
        live = jnp.arange(UPD_DEV, dtype=jnp.int32) < piece_count
        cross_rows = jnp.where(live, (section_first + piece_owner) * ROWS_DEV + piece_target, total_rows).astype(jnp.int32)
        local_rows = (device * ROWS_DEV + own_target).astype(jnp.int32)
        updated = updated.at[cross_rows].add(-cross_blocks.astype(jnp.float32), mode="drop")
        updated = updated.at[local_rows].add(-local_blocks.astype(jnp.float32))
        return updated, None

    updated, unused = lax.scan(per_device, coupling.astype(jnp.float32), inputs)
    step_matrix = -jnp.einsum("kab,kbc->kac", diag_inverse, updated, precision=precise)
    step_offset = jnp.einsum("kab,knb->kna", diag_inverse, adjoint_seed, precision=precise)
    per_section = N_ROW * ROWS_DEV
    section_matrix = step_matrix.reshape(N_SECTION, per_section, width, width)
    section_offset = step_offset.reshape(N_SECTION, per_section, NRHS, width)

    def backward(later, pieces):
        matrix, vector = pieces
        current = vector + jnp.einsum("kab,knb->kna", matrix, later, precision=precise)
        return current, current

    closing_state, adjoint = lax.scan(backward, jnp.zeros((per_section, NRHS, width), jnp.float32), (section_matrix, section_offset), reverse=True)
    return updated, adjoint.reshape(total_rows, NRHS, width)
```

```python
import functools

import jax
import jax.numpy as jnp
from jax import lax
from jax.experimental import pallas as pl
from jax.experimental.pallas import tpu as pltpu
from jax.sharding import PartitionSpec as P

STEP = 16
DEPTH = 4
HIGH = 4
LAG = 2
VMEM_LIMIT = 56 * 1024 * 1024
precise = lax.Precision.HIGHEST
MESH = pl.DeviceIdType.MESH


def products_kernel(
    low, rows, cpiv, cown, crow, ccount, lpiv, lrow,
    cl, cr, ll, lr, pinv, coup, part, base, acc,
):
    g = pl.program_id(0)
    targets = part.shape[0]

    @pl.when(g == 0)
    def _():
        def clear(i, carry):
            acc[i] = jnp.zeros(acc.shape[1:], acc.dtype)
            return carry

        lax.fori_loop(0, targets, clear, 0)
        base[...] = coup[...].astype(jnp.float32)

    live = ccount[0]
    for i in range(STEP):
        t = g * STEP + i
        owner = cown[t]
        spot = ((owner % low) * rows + crow[t]) * HIGH + owner // low
        spot = jnp.where(t < live, spot, targets)
        scaled = jnp.dot(cl[i], pinv[cpiv[t]], preferred_element_type=jnp.float32)
        update = jnp.dot(
            scaled.astype(jnp.bfloat16), cr[i], preferred_element_type=jnp.float32
        )
        acc[spot] += update
        scaled = jnp.dot(ll[i], pinv[lpiv[t]], preferred_element_type=jnp.float32)
        update = jnp.dot(
            scaled.astype(jnp.bfloat16), lr[i], preferred_element_type=jnp.float32
        )
        base[lrow[t]] -= update

    @pl.when(g == pl.num_programs(0) - 1)
    def _():
        def put(i, carry):
            part[i] = acc[i].astype(part.dtype)
            return carry

        lax.fori_loop(0, targets, put, 0)


def exchange_kernel(
    low, sections, part, base, diag, seed, new, adj,
    own, got_low, got_high, later, matrix,
    load_sem, ls, lr, hs, hr, vs, vr,
):
    rows = base.shape[0]
    row = lax.axis_index("row")
    sec = lax.axis_index("section")
    hi, lo = row // low, row % low

    load = pltpu.make_async_copy(part.at[lo], own, load_sem)
    load.start()

    barrier = pltpu.get_barrier_semaphore()
    for d in range(1, low):
        peer = hi * low + (lo + d) % low
        pl.semaphore_signal(barrier, inc=1, device_id={"row": peer}, device_id_type=MESH)
    for d in range(1, HIGH):
        peer = ((hi + d) % HIGH) * low + lo
        pl.semaphore_signal(barrier, inc=1, device_id={"row": peer}, device_id_type=MESH)

    @pl.when(sec > 0)
    def _():
        pl.semaphore_signal(
            barrier, inc=1, device_id={"section": sec - 1}, device_id_type=MESH
        )

    @pl.when(sec < sections - 1)
    def _():
        pl.semaphore_signal(
            barrier, inc=1, device_id={"section": sec + 1}, device_id_type=MESH
        )

    ends = jnp.where(sec > 0, 1, 0) + jnp.where(sec < sections - 1, 1, 0)
    pl.semaphore_wait(barrier, (low - 1) + (HIGH - 1) + ends)

    def low_copy(d, k):
        peer = (lo + d) % low
        return pltpu.make_async_remote_copy(
            src_ref=part.at[peer, k],
            dst_ref=got_low.at[d - 1, k],
            send_sem=ls.at[d - 1, k],
            recv_sem=lr.at[d - 1, k],
            device_id={"row": hi * low + peer},
            device_id_type=MESH,
        )

    def high_copy(d, k):
        peer = (hi + d) % HIGH
        return pltpu.make_async_remote_copy(
            src_ref=own.at[k, peer],
            dst_ref=got_high.at[d - 1, k],
            send_sem=hs.at[d - 1, k],
            recv_sem=hr.at[d - 1, k],
            device_id={"row": peer * low + lo},
            device_id_type=MESH,
        )

    def chain_copy(k, target):
        return pltpu.make_async_remote_copy(
            src_ref=adj.at[k],
            dst_ref=later.at[k],
            send_sem=vs.at[k],
            recv_sem=vr.at[k],
            device_id={"section": target},
            device_id_type=MESH,
        )

    for k in range(DEPTH):
        for d in range(1, low):
            low_copy(d, k).start()

    def offset(k, carry):
        adj[k] = lax.dot_general(
            seed[k], diag[k], (((1,), (1,)), ((), ())),
            precision=precise, preferred_element_type=jnp.float32,
        )

        @pl.when(sec == sections - 1)
        def _():
            chain_copy(k, sec - 1).start()

        return carry

    lax.fori_loop(0, rows, offset, 0)
    load.wait()

    def step(c, carry):
        @pl.when(c + DEPTH < rows)
        def _():
            for d in range(1, low):
                low_copy(d, c + DEPTH).start()

        @pl.when(c < rows)
        def _():
            for d in range(1, low):
                low_copy(d, c).wait_recv()
            for h in range(HIGH):
                total = own[c, h].astype(jnp.float32)
                for d in range(1, low):
                    total += got_low[d - 1, c, h].astype(jnp.float32)
                own[c, h] = total.astype(own.dtype)
            for d in range(1, HIGH):
                high_copy(d, c).start()

        j = c - LAG

        @pl.when((j >= 0) & (j < rows))
        def _():
            for d in range(1, HIGH):
                high_copy(d, j).wait_recv()
            total = own[j, hi].astype(jnp.float32)
            for d in range(1, HIGH):
                total += got_high[d - 1, j].astype(jnp.float32)
            total = base[j] - total
            new[j] = total
            matrix[j] = jnp.dot(
                diag[j], total, precision=precise, preferred_element_type=jnp.float32
            )

        m = c - LAG - (sections - 2 - sec)

        @pl.when((sec < sections - 1) & (m >= 0) & (m < rows))
        def _():
            chain_copy(m, sec).wait_recv()
            adj[m] -= lax.dot_general(
                later[m], matrix[m], (((1,), (1,)), ((), ())),
                precision=precise, preferred_element_type=jnp.float32,
            )

            @pl.when(sec > 0)
            def _():
                chain_copy(m, sec - 1).start()

        return carry

    lax.fori_loop(0, rows + LAG + sections - 2, step, 0)

    def drain(k, carry):
        for d in range(1, low):
            low_copy(d, k).wait_send()
        for d in range(1, HIGH):
            high_copy(d, k).wait_send()

        @pl.when(sec > 0)
        def _():
            chain_copy(k, sec - 1).wait_send()

        return carry

    lax.fori_loop(0, rows, drain, 0)


def per_device(
    coupling,
    diag_inverse,
    pivot_inverse,
    cross_left,
    cross_right,
    cross_pivot,
    cross_owner,
    foreign_target_row,
    cross_count,
    local_left,
    local_right,
    local_pivot,
    local_target,
    adjoint_seed,
):
    rows, width, _ = coupling.shape
    groups = lax.axis_size("row")
    sections = lax.axis_size("section")
    low = groups // HIGH
    slots = cross_left.shape[0]
    targets = groups * rows
    block = (width, width)

    def whole(shape):
        return pl.BlockSpec(shape, lambda g, *_: (0,) * len(shape))

    def streamed():
        return pl.BlockSpec((STEP,) + block, lambda g, *_: (g, 0, 0))

    part, base = pl.pallas_call(
        functools.partial(products_kernel, low, rows),
        out_shape=(
            jax.ShapeDtypeStruct((targets,) + block, jnp.bfloat16),
            jax.ShapeDtypeStruct((rows,) + block, jnp.float32),
        ),
        grid_spec=pltpu.PrefetchScalarGridSpec(
            num_scalar_prefetch=6,
            grid=(slots // STEP,),
            in_specs=[streamed(), streamed(), streamed(), streamed(),
                      whole(pivot_inverse.shape), whole(coupling.shape)],
            out_specs=[whole((targets,) + block), whole((rows,) + block)],
            scratch_shapes=[pltpu.VMEM((targets + 1,) + block, jnp.float32)],
        ),
        compiler_params=pltpu.CompilerParams(
            dimension_semantics=("arbitrary",), vmem_limit_bytes=VMEM_LIMIT
        ),
        cost_estimate=pl.CostEstimate(
            flops=8 * slots * width ** 3, bytes_accessed=22 * 1024 * 1024, transcendentals=0
        ),
        name="products",
    )(cross_pivot, cross_owner[:, 0], foreign_target_row, cross_count, local_pivot,
      local_target, cross_left, cross_right, local_left, local_right, pivot_inverse, coupling)

    part = part.reshape((low, rows, HIGH) + block)
    vmem = pl.BlockSpec(memory_space=pltpu.VMEM)
    dma = pltpu.SemaphoreType.DMA
    return pl.pallas_call(
        functools.partial(exchange_kernel, low, sections),
        out_shape=(
            jax.ShapeDtypeStruct((rows,) + block, jnp.float32),
            jax.ShapeDtypeStruct((rows,) + block, jnp.float32),
        ),
        in_specs=[pl.BlockSpec(memory_space=pl.ANY), vmem, vmem, vmem],
        out_specs=(vmem, vmem),
        scratch_shapes=[
            pltpu.VMEM((rows, HIGH) + block, jnp.bfloat16),
            pltpu.VMEM((low - 1, rows, HIGH) + block, jnp.bfloat16),
            pltpu.VMEM((HIGH - 1, rows) + block, jnp.bfloat16),
            pltpu.VMEM((rows,) + block, jnp.float32),
            pltpu.VMEM((rows,) + block, jnp.float32),
            dma(()),
            dma((low - 1, rows)),
            dma((low - 1, rows)),
            dma((HIGH - 1, rows)),
            dma((HIGH - 1, rows)),
            dma((rows,)),
            dma((rows,)),
        ],
        compiler_params=pltpu.CompilerParams(
            collective_id=0, has_side_effects=True, vmem_limit_bytes=VMEM_LIMIT
        ),
        name="exchange",
    )(part, base, diag_inverse, adjoint_seed)


def solution(mesh):
    spread = P(("section", "row"))
    return jax.shard_map(
        per_device,
        mesh=mesh,
        in_specs=(spread,) * 14,
        out_specs=(spread, spread),
        check_vma=False,
    )
```

```python
import functools

import jax
import jax.numpy as jnp
from jax import lax
from jax.experimental import pallas as pl
from jax.experimental.pallas import tpu as pltpu
from jax.sharding import PartitionSpec as P

STEP = 16
GROUP = 4
LOCAL_GROUP = 4
DEPTH = 4
HIGH = 4
LAG = 2
VMEM_LIMIT = 56 * 1024 * 1024
precise = lax.Precision.HIGHEST
MESH = pl.DeviceIdType.MESH


def products_kernel(
    low, rows, cpiv, cown, crow, ccount, lpiv, lrow,
    cl, cr, pinv, part, index, acc,
):
    g = pl.program_id(0)
    targets = part.shape[0]

    @pl.when(g == 0)
    def _():
        def clear(i, carry):
            acc[i] = jnp.zeros(acc.shape[1:], acc.dtype)
            return carry

        lax.fori_loop(0, targets, clear, 0)
        index[...] = local_order(lpiv[...], lrow[...])

    live = ccount[0]
    for first in range(0, STEP, GROUP):
        picked = range(first, first + GROUP)
        scaled = [
            jnp.dot(
                cl[i], pinv[cpiv[g * STEP + i]], preferred_element_type=jnp.float32
            ).astype(jnp.bfloat16)
            for i in picked
        ]
        updates = [
            jnp.dot(half, cr[i], preferred_element_type=jnp.float32)
            for half, i in zip(scaled, picked)
        ]
        for update, i in zip(updates, picked):
            t = g * STEP + i
            owner = cown[t]
            spot = ((owner % low) * rows + crow[t]) * HIGH + owner // low
            acc[jnp.where(t < live, spot, targets)] += update

    @pl.when(g == pl.num_programs(0) - 1)
    def _():
        def put(i, carry):
            part[i] = acc[i].astype(part.dtype)
            return carry

        lax.fori_loop(0, targets, put, 0)


def local_order(pivot, row):
    n = row.shape[1]
    lane = lax.broadcasted_iota(jnp.int32, (n, n), 1).astype(jnp.float32)
    slot = lax.broadcasted_iota(jnp.int32, (n, n), 0).astype(jnp.float32)

    def down(x):
        return jnp.broadcast_to(x, (n, n)).T

    def total(x):
        return jnp.sum(x, axis=0, keepdims=True)

    row = row.astype(jnp.float32)
    key = row * n + lane[:1]
    rank = total(jnp.where(down(key) < key, 1.0, 0.0))
    hit = down(rank) == lane
    rows_down = down(row)
    order = total(jnp.where(hit, slot, 0.0))
    pivots = total(jnp.where(hit, down(pivot.astype(jnp.float32)), 0.0))
    sorted_rows = total(jnp.where(hit, rows_down, 0.0))
    last = total(jnp.where(rows_down <= lane, 1.0, 0.0)) - 1.0
    count = total(jnp.where(rows_down == lane, 1.0, 0.0))
    blank = jnp.zeros((3, n), jnp.float32)
    return jnp.concatenate(
        [order, pivots, sorted_rows, last, count, blank], axis=0
    ).astype(jnp.int32)


def results_kernel(new_in, adj_in, new_out, adj_out, sems):
    pieces = sems.shape[1]
    size = new_in.shape[0] // pieces
    copies = []
    for a, (source, target) in enumerate(((new_in, new_out), (adj_in, adj_out))):
        for p in range(pieces):
            span = pl.ds(p * size, size)
            copies.append(
                pltpu.make_async_copy(source.at[span], target.at[span], sems.at[a, p])
            )
    for copy in copies:
        copy.start()
    for copy in copies:
        copy.wait()


def exchange_kernel(
    low, sections, index, part, coup_hbm, diag_hbm, seed_hbm, pinv_hbm, left_hbm, right_hbm,
    new, adj,
    own, got_low, got_high, later, matrix,
    base, coup, diag, seed, pinv, left, right, sums,
    load_sem, ls, lr, hs, hr, vs, vr,
):
    rows, width, _ = base.shape
    slots = left.shape[0]
    row = lax.axis_index("row")
    sec = lax.axis_index("section")
    hi, lo = row // low, row % low

    loads = [
        pltpu.make_async_copy(source, target, load_sem.at[i])
        for i, (source, target) in enumerate((
            (seed_hbm, seed), (diag_hbm, diag), (pinv_hbm, pinv), (left_hbm, left),
            (right_hbm, right), (coup_hbm, coup), (part.at[lo], own),
        ))
    ]

    barrier = pltpu.get_barrier_semaphore()
    for d in range(1, low):
        peer = hi * low + (lo + d) % low
        pl.semaphore_signal(barrier, inc=1, device_id={"row": peer}, device_id_type=MESH)
    for d in range(1, HIGH):
        peer = ((hi + d) % HIGH) * low + lo
        pl.semaphore_signal(barrier, inc=1, device_id={"row": peer}, device_id_type=MESH)

    @pl.when(sec > 0)
    def _():
        pl.semaphore_signal(
            barrier, inc=1, device_id={"section": sec - 1}, device_id_type=MESH
        )

    @pl.when(sec < sections - 1)
    def _():
        pl.semaphore_signal(
            barrier, inc=1, device_id={"section": sec + 1}, device_id_type=MESH
        )

    ends = jnp.where(sec > 0, 1, 0) + jnp.where(sec < sections - 1, 1, 0)
    pl.semaphore_wait(barrier, (low - 1) + (HIGH - 1) + ends)

    def low_copy(d, k):
        peer = (lo + d) % low
        return pltpu.make_async_remote_copy(
            src_ref=part.at[peer, k],
            dst_ref=got_low.at[d - 1, k],
            send_sem=ls.at[d - 1, k],
            recv_sem=lr.at[d - 1, k],
            device_id={"row": hi * low + peer},
            device_id_type=MESH,
        )

    def high_copy(d, k):
        peer = (hi + d) % HIGH
        return pltpu.make_async_remote_copy(
            src_ref=own.at[k, peer],
            dst_ref=got_high.at[d - 1, k],
            send_sem=hs.at[d - 1, k],
            recv_sem=hr.at[d - 1, k],
            device_id={"row": peer * low + lo},
            device_id_type=MESH,
        )

    def chain_copy(k, target):
        return pltpu.make_async_remote_copy(
            src_ref=adj.at[k],
            dst_ref=later.at[k],
            send_sem=vs.at[k],
            recv_sem=vr.at[k],
            device_id={"section": target},
            device_id_type=MESH,
        )

    for k in range(DEPTH):
        for d in range(1, low):
            low_copy(d, k).start()

    for load in loads:
        load.start()
    loads[0].wait()
    loads[1].wait()

    def offset(k, carry):
        adj[k] = lax.dot_general(
            seed[k], diag[k], (((1,), (1,)), ((), ())),
            precision=precise, preferred_element_type=jnp.float32,
        )

        @pl.when(sec == sections - 1)
        def _():
            chain_copy(k, sec - 1).start()

        return carry

    lax.fori_loop(0, rows, offset, 0)
    for load in loads[2:]:
        load.wait()

    def local_group(g, run):
        at = [g * LOCAL_GROUP + i for i in range(LOCAL_GROUP)]
        scaled = [
            jnp.dot(
                left[index[0, j]], pinv[index[1, j]], preferred_element_type=jnp.float32
            ).astype(jnp.bfloat16)
            for j in at
        ]
        updates = [
            jnp.dot(half, right[index[0, j]], preferred_element_type=jnp.float32)
            for half, j in zip(scaled, at)
        ]
        for update, j in zip(updates, at):
            same = index[2, j] == index[2, jnp.maximum(j - 1, 0)]
            run = run * jnp.where(same, 1.0, 0.0) + update
            sums[j] = run
        return run

    lax.fori_loop(
        0, slots // LOCAL_GROUP, local_group, jnp.zeros((width, width), jnp.float32)
    )

    def local_row(k, carry):
        used = jnp.where(index[4, k] > 0, 1.0, 0.0)
        total = sums[jnp.maximum(index[3, k], 0)] * used
        base[k] = coup[k].astype(jnp.float32) - total
        return carry

    lax.fori_loop(0, rows, local_row, 0)

    def step(c, carry):
        @pl.when(c + DEPTH < rows)
        def _():
            for d in range(1, low):
                low_copy(d, c + DEPTH).start()

        @pl.when(c < rows)
        def _():
            for d in range(1, low):
                low_copy(d, c).wait_recv()
            for h in range(HIGH):
                total = own[c, h].astype(jnp.float32)
                for d in range(1, low):
                    total += got_low[d - 1, c, h].astype(jnp.float32)
                own[c, h] = total.astype(own.dtype)
            for d in range(1, HIGH):
                high_copy(d, c).start()

        j = c - LAG

        @pl.when((j >= 0) & (j < rows))
        def _():
            for d in range(1, HIGH):
                high_copy(d, j).wait_recv()
            total = own[j, hi].astype(jnp.float32)
            for d in range(1, HIGH):
                total += got_high[d - 1, j].astype(jnp.float32)
            total = base[j] - total
            new[j] = total
            matrix[j] = jnp.dot(
                diag[j], total, precision=precise, preferred_element_type=jnp.float32
            )

        m = c - LAG - (sections - 2 - sec)

        @pl.when((sec < sections - 1) & (m >= 0) & (m < rows))
        def _():
            chain_copy(m, sec).wait_recv()
            adj[m] -= lax.dot_general(
                later[m], matrix[m], (((1,), (1,)), ((), ())),
                precision=precise, preferred_element_type=jnp.float32,
            )

            @pl.when(sec > 0)
            def _():
                chain_copy(m, sec - 1).start()

        return carry

    lax.fori_loop(0, rows + LAG + sections - 2, step, 0)

    def drain(k, carry):
        for d in range(1, low):
            low_copy(d, k).wait_send()
        for d in range(1, HIGH):
            high_copy(d, k).wait_send()

        @pl.when(sec > 0)
        def _():
            chain_copy(k, sec - 1).wait_send()

        return carry

    lax.fori_loop(0, rows, drain, 0)


def per_device(
    coupling,
    diag_inverse,
    pivot_inverse,
    cross_left,
    cross_right,
    cross_pivot,
    cross_owner,
    foreign_target_row,
    cross_count,
    local_left,
    local_right,
    local_pivot,
    local_target,
    adjoint_seed,
):
    rows, width, _ = coupling.shape
    groups = lax.axis_size("row")
    sections = lax.axis_size("section")
    low = groups // HIGH
    slots, local_slots = cross_left.shape[0], local_left.shape[0]
    targets = groups * rows
    block = (width, width)

    def whole(shape):
        return pl.BlockSpec(shape, lambda g, *_: (0,) * len(shape))

    def streamed():
        return pl.BlockSpec((STEP,) + block, lambda g, *_: (g, 0, 0))

    part, index = pl.pallas_call(
        functools.partial(products_kernel, low, rows),
        out_shape=(
            jax.ShapeDtypeStruct((targets,) + block, jnp.bfloat16),
            jax.ShapeDtypeStruct((8, local_slots), jnp.int32),
        ),
        grid_spec=pltpu.PrefetchScalarGridSpec(
            num_scalar_prefetch=4,
            grid=(slots // STEP,),
            in_specs=[whole((1, local_slots)), whole((1, local_slots)),
                      streamed(), streamed(), whole(pivot_inverse.shape)],
            out_specs=[whole((targets,) + block), whole((8, local_slots))],
            scratch_shapes=[pltpu.VMEM((targets + 1,) + block, jnp.float32)],
        ),
        compiler_params=pltpu.CompilerParams(
            dimension_semantics=("arbitrary",), vmem_limit_bytes=VMEM_LIMIT
        ),
        cost_estimate=pl.CostEstimate(
            flops=4 * slots * width ** 3, bytes_accessed=12 * 1024 * 1024, transcendentals=0
        ),
        name="products",
    )(cross_pivot, cross_owner[:, 0], foreign_target_row, cross_count,
      local_pivot.reshape(1, local_slots), local_target.reshape(1, local_slots),
      cross_left, cross_right, pivot_inverse)

    part = part.reshape((low, rows, HIGH) + block)
    vmem = pl.BlockSpec(memory_space=pltpu.VMEM)
    hbm = pl.BlockSpec(memory_space=pl.ANY)
    dma = pltpu.SemaphoreType.DMA
    outs = (
        jax.ShapeDtypeStruct((rows,) + block, jnp.float32),
        jax.ShapeDtypeStruct((rows,) + block, jnp.float32),
    )
    results = pl.pallas_call(
        functools.partial(exchange_kernel, low, sections),
        out_shape=outs,
        in_specs=[pl.BlockSpec(memory_space=pltpu.SMEM)] + [hbm] * 7,
        out_specs=(vmem, vmem),
        scratch_shapes=[
            pltpu.VMEM((rows, HIGH) + block, jnp.bfloat16),
            pltpu.VMEM((low - 1, rows, HIGH) + block, jnp.bfloat16),
            pltpu.VMEM((HIGH - 1, rows) + block, jnp.bfloat16),
            pltpu.VMEM((rows,) + block, jnp.float32),
            pltpu.VMEM((rows,) + block, jnp.float32),
            pltpu.VMEM((rows,) + block, jnp.float32),
            pltpu.VMEM(coupling.shape, coupling.dtype),
            pltpu.VMEM(diag_inverse.shape, jnp.float32),
            pltpu.VMEM(adjoint_seed.shape, jnp.float32),
            pltpu.VMEM(pivot_inverse.shape, pivot_inverse.dtype),
            pltpu.VMEM(local_left.shape, local_left.dtype),
            pltpu.VMEM(local_right.shape, local_right.dtype),
            pltpu.VMEM((local_slots,) + block, jnp.float32),
            dma((7,)),
            dma((low - 1, rows)),
            dma((low - 1, rows)),
            dma((HIGH - 1, rows)),
            dma((HIGH - 1, rows)),
            dma((rows,)),
            dma((rows,)),
        ],
        compiler_params=pltpu.CompilerParams(
            collective_id=0, has_side_effects=True, vmem_limit_bytes=VMEM_LIMIT
        ),
        name="exchange",
    )(index, part, coupling, diag_inverse, adjoint_seed, pivot_inverse, local_left, local_right)
    return pl.pallas_call(
        results_kernel,
        out_shape=outs,
        in_specs=[hbm, hbm],
        out_specs=(hbm, hbm),
        scratch_shapes=[dma((2, 4))],
        compiler_params=pltpu.CompilerParams(vmem_limit_bytes=VMEM_LIMIT),
        name="results",
    )(*results)


def solution(mesh):
    spread = P(("section", "row"))
    return jax.shard_map(
        per_device,
        mesh=mesh,
        in_specs=(spread,) * 14,
        out_specs=(spread, spread),
        check_vma=False,
    )
```

```python
import functools

import jax
import jax.numpy as jnp
from jax import lax
from jax.experimental import pallas as pl
from jax.experimental.pallas import tpu as pltpu
from jax.sharding import PartitionSpec as P

STEP = 32
GROUP = 4
LOCAL_GROUP = 4
DEPTH = 4
HIGH = 4
LAG = 2
LOCAL_STEPS = 4
WRITES = 8
VMEM_LIMIT = 56 * 1024 * 1024
MESH = pl.DeviceIdType.MESH


def products_kernel(
    low, rows, cpiv, cown, crow, ccount, lpiv, lrow,
    cl, cr, pinv, part, index, acc, rounded, sems,
):
    g = pl.program_id(0)
    targets = part.shape[0]

    @pl.when(g == 0)
    def _():
        def clear(i, carry):
            acc[i] = jnp.zeros(acc.shape[1:], acc.dtype)
            return carry

        lax.fori_loop(0, targets, clear, 0, unroll=8)
        index[...] = local_order(lpiv[...], lrow[...])

    live = ccount[0]
    for first in range(0, STEP, GROUP):
        picked = range(first, first + GROUP)
        scaled = [
            jnp.dot(
                cl[i], pinv[cpiv[g * STEP + i]], preferred_element_type=jnp.float32
            ).astype(jnp.bfloat16)
            for i in picked
        ]
        updates = [
            jnp.dot(half, cr[i], preferred_element_type=jnp.float32)
            for half, i in zip(scaled, picked)
        ]
        for update, i in zip(updates, picked):
            t = g * STEP + i
            owner = cown[t]
            spot = ((owner % low) * rows + crow[t]) * HIGH + owner // low
            acc[jnp.where(t < live, spot, targets)] += update

    @pl.when(g == pl.num_programs(0) - 1)
    def _():
        size = targets // WRITES

        def write(n):
            span = pl.ds(n * size, size)
            return pltpu.make_async_copy(rounded.at[span], part.at[span], sems.at[n])

        for n in range(WRITES):

            def put(i, carry):
                rounded[n * size + i] = acc[n * size + i].astype(rounded.dtype)
                return carry

            lax.fori_loop(0, size, put, 0, unroll=8)
            write(n).start()
        for n in range(WRITES):
            write(n).wait()


def local_order(pivot, row):
    n = row.shape[1]
    lane = lax.broadcasted_iota(jnp.int32, (n, n), 1).astype(jnp.float32)
    slot = lax.broadcasted_iota(jnp.int32, (n, n), 0).astype(jnp.float32)

    def down(x):
        return jnp.broadcast_to(x, (n, n)).T

    def total(x):
        return jnp.sum(x, axis=0, keepdims=True)

    row = row.astype(jnp.float32)
    key = row * n + lane[:1]
    rank = total(jnp.where(down(key) < key, 1.0, 0.0))
    hit = down(rank) == lane
    rows_down = down(row)
    order = total(jnp.where(hit, slot, 0.0))
    pivots = total(jnp.where(hit, down(pivot.astype(jnp.float32)), 0.0))
    sorted_rows = total(jnp.where(hit, rows_down, 0.0))
    last = total(jnp.where(rows_down <= lane, 1.0, 0.0)) - 1.0
    count = total(jnp.where(rows_down == lane, 1.0, 0.0))
    blank = jnp.zeros((3, n), jnp.float32)
    return jnp.concatenate(
        [order, pivots, sorted_rows, last, count, blank], axis=0
    ).astype(jnp.int32)


def results_kernel(new_in, adj_in, new_out, adj_out, held, in_sems, out_sems):
    pieces = in_sems.shape[1]
    size = new_in.shape[0] // pieces
    reads, writes = [], []
    for a, (source, target) in enumerate(((new_in, new_out), (adj_in, adj_out))):
        for p in range(pieces):
            span = pl.ds(p * size, size)
            reads.append(
                pltpu.make_async_copy(source.at[span], held.at[a, span], in_sems.at[a, p])
            )
            writes.append(
                pltpu.make_async_copy(held.at[a, span], target.at[span], out_sems.at[a, p])
            )
    for read in reads:
        read.start()
    for read, write in zip(reads, writes):
        read.wait()
        write.start()
    for write in writes:
        write.wait()


def split(x):
    high = x.astype(jnp.bfloat16)
    return high, (x - high.astype(jnp.float32)).astype(jnp.bfloat16)


def three_products(left, right, contract):
    def one(a, b):
        return lax.dot_general(a, b, (contract, ((), ())), preferred_element_type=jnp.float32)

    return one(left[0], right[0]) + (one(left[0], right[1]) + one(left[1], right[0]))


def exchange_kernel(
    low, sections, index, part, coup_hbm, diag_hbm, seed_hbm, pinv_hbm, left_hbm, right_hbm,
    new_hbm, adj_hbm,
    own, got_low, got_high, later, matrix_high, matrix_low, new, adj,
    base, coup, diag, seed, pinv, left, right, sums, running,
    load_sem, ls, lr, hs, hr, vs, vr, ns, ads,
):
    rows, width, _ = base.shape
    slots = left.shape[0]
    row = lax.axis_index("row")
    sec = lax.axis_index("section")
    hi, lo = row // low, row % low

    loads = [
        pltpu.make_async_copy(source, target, load_sem.at[i])
        for i, (source, target) in enumerate((
            (part.at[lo], own), (seed_hbm, seed), (diag_hbm, diag), (pinv_hbm, pinv),
            (left_hbm, left), (right_hbm, right), (coup_hbm, coup),
        ))
    ]

    barrier = pltpu.get_barrier_semaphore()
    for d in range(1, low):
        peer = hi * low + (lo + d) % low
        pl.semaphore_signal(barrier, inc=1, device_id={"row": peer}, device_id_type=MESH)
    for d in range(1, HIGH):
        peer = ((hi + d) % HIGH) * low + lo
        pl.semaphore_signal(barrier, inc=1, device_id={"row": peer}, device_id_type=MESH)

    @pl.when(sec > 0)
    def _():
        pl.semaphore_signal(
            barrier, inc=1, device_id={"section": sec - 1}, device_id_type=MESH
        )

    @pl.when(sec < sections - 1)
    def _():
        pl.semaphore_signal(
            barrier, inc=1, device_id={"section": sec + 1}, device_id_type=MESH
        )

    ends = jnp.where(sec > 0, 1, 0) + jnp.where(sec < sections - 1, 1, 0)
    pl.semaphore_wait(barrier, (low - 1) + (HIGH - 1) + ends)

    def low_copy(d, k):
        peer = (lo + d) % low
        return pltpu.make_async_remote_copy(
            src_ref=part.at[peer, k],
            dst_ref=got_low.at[d - 1, k],
            send_sem=ls.at[d - 1, k],
            recv_sem=lr.at[d - 1, k],
            device_id={"row": hi * low + peer},
            device_id_type=MESH,
        )

    def high_copy(d, k):
        peer = (hi + d) % HIGH
        return pltpu.make_async_remote_copy(
            src_ref=own.at[k, peer],
            dst_ref=got_high.at[d - 1, k],
            send_sem=hs.at[d - 1, k],
            recv_sem=hr.at[d - 1, k],
            device_id={"row": peer * low + lo},
            device_id_type=MESH,
        )

    def chain_copy(k, target):
        return pltpu.make_async_remote_copy(
            src_ref=adj.at[k],
            dst_ref=later.at[k],
            send_sem=vs.at[k],
            recv_sem=vr.at[k],
            device_id={"section": target},
            device_id_type=MESH,
        )

    for k in range(DEPTH):
        for d in range(1, low):
            low_copy(d, k).start()

    for load in loads:
        load.start()
    running[...] = jnp.zeros_like(running)
    loads[0].wait()

    def new_write(k):
        return pltpu.make_async_copy(new.at[k], new_hbm.at[k], ns.at[k])

    def adj_write(k):
        return pltpu.make_async_copy(adj.at[k], adj_hbm.at[k], ads.at[k])

    def local_group(g, run):
        at = [g * LOCAL_GROUP + i for i in range(LOCAL_GROUP)]
        scaled = [
            jnp.dot(
                left[index[0, j]], pinv[index[1, j]], preferred_element_type=jnp.float32
            ).astype(jnp.bfloat16)
            for j in at
        ]
        updates = [
            jnp.dot(half, right[index[0, j]], preferred_element_type=jnp.float32)
            for half, j in zip(scaled, at)
        ]
        for update, j in zip(updates, at):
            same = index[2, j] == index[2, jnp.maximum(j - 1, 0)]
            run = run * jnp.where(same, 1.0, 0.0) + update
            sums[j] = run
        return run

    def local_row(k, carry):
        used = jnp.where(index[4, k] > 0, 1.0, 0.0)
        total = sums[jnp.maximum(index[3, k], 0)] * used
        base[k] = coup[k].astype(jnp.float32) - total
        return carry

    def finish_row(j, carry):
        for d in range(1, HIGH):
            high_copy(d, j).wait_recv()
        total = own[j, hi].astype(jnp.float32)
        for d in range(1, HIGH):
            total += got_high[d - 1, j].astype(jnp.float32)
        total = base[j] - total
        new[j] = total
        new_write(j).start()
        matrix_high[j], matrix_low[j] = split(
            three_products(split(diag[j]), split(total), ((1,), (0,)))
        )
        return carry

    def solve_row(m, carry):
        chain_copy(m, sec).wait_recv()
        adj[m] -= three_products(
            split(later[m]), (matrix_high[m], matrix_low[m]), ((1,), (1,))
        )

        @pl.when(sec > 0)
        def _():
            chain_copy(m, sec - 1).start()

        adj_write(m).start()
        return carry

    def finished(c):
        return jnp.where(c < LOCAL_STEPS, 0, jnp.clip(c - LAG + 1, 0, rows))


    def step(c, carry):
        @pl.when(c + DEPTH < rows)
        def _():
            for d in range(1, low):
                low_copy(d, c + DEPTH).start()

        @pl.when(c < rows)
        def _():
            for d in range(1, low):
                low_copy(d, c).wait_recv()
            for h in range(HIGH):
                total = own[c, h].astype(jnp.float32)
                for d in range(1, low):
                    total += got_low[d - 1, c, h].astype(jnp.float32)
                own[c, h] = total.astype(own.dtype)
            for d in range(1, HIGH):
                high_copy(d, c).start()

        @pl.when(c == 0)
        def _():
            for load in loads[1:]:
                load.wait()

        @pl.when(c < rows)
        def _():
            adj[c] = three_products(split(seed[c]), split(diag[c]), ((1,), (1,)))

        @pl.when((c < rows) & (sec == sections - 1))
        def _():
            chain_copy(c, sec - 1).start()
            adj_write(c).start()

        @pl.when(c < LOCAL_STEPS)
        def _():
            per_step = slots // (LOCAL_STEPS * LOCAL_GROUP)
            running[...] = lax.fori_loop(
                c * per_step, (c + 1) * per_step, local_group, running[...]
            )

        @pl.when(c == LOCAL_STEPS - 1)
        def _():
            lax.fori_loop(0, rows, local_row, 0)

        lax.fori_loop(finished(c - 1), finished(c), finish_row, 0)
        delay = sections - 2 - sec

        @pl.when(sec < sections - 1)
        def _():
            lax.fori_loop(finished(c - 1 - delay), finished(c - delay), solve_row, 0)

        return carry

    lax.fori_loop(0, rows + LAG + sections - 2, step, 0)

    def drain(k, carry):
        new_write(k).wait()
        adj_write(k).wait()
        for d in range(1, low):
            low_copy(d, k).wait_send()
        for d in range(1, HIGH):
            high_copy(d, k).wait_send()

        @pl.when(sec > 0)
        def _():
            chain_copy(k, sec - 1).wait_send()

        return carry

    lax.fori_loop(0, rows, drain, 0)


def per_device(
    coupling,
    diag_inverse,
    pivot_inverse,
    cross_left,
    cross_right,
    cross_pivot,
    cross_owner,
    foreign_target_row,
    cross_count,
    local_left,
    local_right,
    local_pivot,
    local_target,
    adjoint_seed,
):
    rows, width, _ = coupling.shape
    groups = lax.axis_size("row")
    sections = lax.axis_size("section")
    low = groups // HIGH
    slots, local_slots = cross_left.shape[0], local_left.shape[0]
    targets = groups * rows
    block = (width, width)

    def whole(shape):
        return pl.BlockSpec(shape, lambda g, *_: (0,) * len(shape))

    def streamed():
        return pl.BlockSpec((STEP,) + block, lambda g, *_: (g, 0, 0))

    part, index = pl.pallas_call(
        functools.partial(products_kernel, low, rows),
        out_shape=(
            jax.ShapeDtypeStruct((targets,) + block, jnp.bfloat16),
            jax.ShapeDtypeStruct((8, local_slots), jnp.int32),
        ),
        grid_spec=pltpu.PrefetchScalarGridSpec(
            num_scalar_prefetch=4,
            grid=(slots // STEP,),
            in_specs=[whole((1, local_slots)), whole((1, local_slots)),
                      streamed(), streamed(), whole(pivot_inverse.shape)],
            out_specs=[pl.BlockSpec(memory_space=pl.ANY), whole((8, local_slots))],
            scratch_shapes=[
                pltpu.VMEM((targets + 1,) + block, jnp.float32),
                pltpu.VMEM((targets,) + block, jnp.bfloat16),
                pltpu.SemaphoreType.DMA((WRITES,)),
            ],
        ),
        compiler_params=pltpu.CompilerParams(
            dimension_semantics=("arbitrary",), vmem_limit_bytes=VMEM_LIMIT
        ),
        cost_estimate=pl.CostEstimate(
            flops=4 * slots * width ** 3, bytes_accessed=12 * 1024 * 1024, transcendentals=0
        ),
        name="products",
    )(cross_pivot, cross_owner[:, 0], foreign_target_row, cross_count,
      local_pivot.reshape(1, local_slots), local_target.reshape(1, local_slots),
      cross_left, cross_right, pivot_inverse)

    part = part.reshape((low, rows, HIGH) + block)
    hbm = pl.BlockSpec(memory_space=pl.ANY)
    dma = pltpu.SemaphoreType.DMA
    outs = (
        jax.ShapeDtypeStruct((rows,) + block, jnp.float32),
        jax.ShapeDtypeStruct((rows,) + block, jnp.float32),
    )
    results = pl.pallas_call(
        functools.partial(exchange_kernel, low, sections),
        out_shape=outs,
        in_specs=[pl.BlockSpec(memory_space=pltpu.SMEM)] + [hbm] * 7,
        out_specs=(hbm, hbm),
        scratch_shapes=[
            pltpu.VMEM((rows, HIGH) + block, jnp.bfloat16),
            pltpu.VMEM((low - 1, rows, HIGH) + block, jnp.bfloat16),
            pltpu.VMEM((HIGH - 1, rows) + block, jnp.bfloat16),
            pltpu.VMEM((rows,) + block, jnp.float32),
            pltpu.VMEM((rows,) + block, jnp.bfloat16),
            pltpu.VMEM((rows,) + block, jnp.bfloat16),
            pltpu.VMEM((rows,) + block, jnp.float32),
            pltpu.VMEM((rows,) + block, jnp.float32),
            pltpu.VMEM((rows,) + block, jnp.float32),
            pltpu.VMEM(coupling.shape, coupling.dtype),
            pltpu.VMEM(diag_inverse.shape, jnp.float32),
            pltpu.VMEM(adjoint_seed.shape, jnp.float32),
            pltpu.VMEM(pivot_inverse.shape, pivot_inverse.dtype),
            pltpu.VMEM(local_left.shape, local_left.dtype),
            pltpu.VMEM(local_right.shape, local_right.dtype),
            pltpu.VMEM((local_slots,) + block, jnp.float32),
            pltpu.VMEM(block, jnp.float32),
            dma((7,)),
            dma((low - 1, rows)),
            dma((low - 1, rows)),
            dma((HIGH - 1, rows)),
            dma((HIGH - 1, rows)),
            dma((rows,)),
            dma((rows,)),
            dma((rows,)),
            dma((rows,)),
        ],
        compiler_params=pltpu.CompilerParams(
            collective_id=0, has_side_effects=True, vmem_limit_bytes=VMEM_LIMIT
        ),
        name="exchange",
    )(index, part, coupling, diag_inverse, adjoint_seed, pivot_inverse, local_left, local_right)
    return pl.pallas_call(
        results_kernel,
        out_shape=outs,
        in_specs=[hbm, hbm],
        out_specs=(hbm, hbm),
        scratch_shapes=[pltpu.VMEM((2, rows) + block, jnp.float32), dma((2, 4)), dma((2, 4))],
        compiler_params=pltpu.CompilerParams(vmem_limit_bytes=VMEM_LIMIT),
        name="results",
    )(*results)


def solution(mesh):
    spread = P(("section", "row"))
    return jax.shard_map(
        per_device,
        mesh=mesh,
        in_specs=(spread,) * 14,
        out_specs=(spread, spread),
        check_vma=False,
    )
```

```python
import functools

import jax
import jax.numpy as jnp
from jax import lax
from jax.experimental import pallas as pl
from jax.experimental.pallas import tpu as pltpu
from jax.sharding import PartitionSpec as P

GROUP = 4
DEPTH = 4
HIGH = 4
LAG = 2
LOCAL_STEPS = 4
CAP = 16
FIRST_PIECES = 4
LANES = 128
VMEM_LIMIT = 56 * 1024 * 1024
MESH = pl.DeviceIdType.MESH


def order_kernel(low, rows, ccount, cpiv, cown, crow, lpiv, lrow, index):
    n = cpiv.shape[1]
    row = lax.axis_index("row")
    hi, lo = row // low, row % low
    lane = lax.broadcasted_iota(jnp.int32, (n, n), 1).astype(jnp.float32)
    slot = lax.broadcasted_iota(jnp.int32, (n, n), 0).astype(jnp.float32)

    def down(x):
        return jnp.broadcast_to(x, (n, n)).T

    def total(x):
        return jnp.sum(x, axis=0, keepdims=True)

    def put(at, x):
        index[at:at + 1, :] = x.astype(jnp.int32)

    def sort(at, key, pivot):
        key_down = down(key)
        spread = key * n + lane[:1]
        rank = total(jnp.where(down(spread) < spread, 1.0, 0.0))
        hit = down(rank) == lane
        put(at, total(jnp.where(hit, slot, 0.0)))
        put(at + 1, total(jnp.where(hit, down(pivot), 0.0)))
        put(at + 2, total(jnp.where(hit, key_down, 0.0)))
        return key_down

    def ends(at, at_count, key_down, first):
        put(at, total(jnp.where(key_down <= lane + first, 1.0, 0.0)) - 1.0)
        put(at_count, total(jnp.where(key_down == lane + first, 1.0, 0.0)))

    local_down = sort(0, lrow[...].astype(jnp.float32), lpiv[...].astype(jnp.float32))
    ends(3, 4, local_down, 0.0)
    owner = cown[...]
    far = ((owner // low) - hi - 1) & (HIGH - 1)
    near = ((owner & (low - 1)) - lo - 1) & (low - 1)
    key = (far * low + near) * rows + crow[...]
    slot_number = lax.broadcasted_iota(jnp.int32, (1, n), 1)
    targets = HIGH * low * rows
    key = jnp.where(slot_number < ccount[0], key, targets)
    cross_down = sort(5, key.astype(jnp.float32), cpiv[...].astype(jnp.float32))
    for p in range(targets // n):
        ends(8 + p, 12 + p, cross_down, float(p * n))


def results_kernel(new_in, adj_in, new_out, adj_out, held, in_sems, out_sems):
    pieces = in_sems.shape[1]
    size = new_in.shape[0] // pieces
    reads, writes = [], []
    for a, (source, target) in enumerate(((new_in, new_out), (adj_in, adj_out))):
        for p in range(pieces):
            span = pl.ds(p * size, size)
            reads.append(
                pltpu.make_async_copy(source.at[span], held.at[a, span], in_sems.at[a, p])
            )
            writes.append(
                pltpu.make_async_copy(held.at[a, span], target.at[span], out_sems.at[a, p])
            )
    for read in reads:
        read.start()
    for read, write in zip(reads, writes):
        read.wait()
        write.start()
    for write in writes:
        write.wait()


def split(x):
    high = x.astype(jnp.bfloat16)
    return high, (x - high.astype(jnp.float32)).astype(jnp.bfloat16)


def three_products(left, right, contract):
    def one(a, b):
        return lax.dot_general(a, b, (contract, ((), ())), preferred_element_type=jnp.float32)

    return one(left[0], right[0]) + (one(left[0], right[1]) + one(left[1], right[0]))


def exchange_kernel(
    low, sections, index, cleft_hbm, cright_hbm, coup_hbm, diag_hbm, seed_hbm, pinv_hbm,
    left_hbm, right_hbm,
    new_hbm, adj_hbm,
    part, got_low, got_high, later, matrix_high, matrix_low, new, adj,
    base, coup, diag, seed, pinv, cleft, cright, left, right, sums, running,
    load_sem, fs, fr, ls, lr, hs, hr, vs, vr, ns, ads,
):
    rows, width, _ = base.shape
    slots = left.shape[0]
    row = lax.axis_index("row")
    sec = lax.axis_index("section")
    hi, lo = row // low, row % low

    loads = [
        pltpu.make_async_copy(source, target, load_sem.at[i])
        for i, (source, target) in enumerate((
            (pinv_hbm, pinv), (cleft_hbm, cleft), (cright_hbm, cright), (seed_hbm, seed),
            (diag_hbm, diag), (left_hbm, left), (right_hbm, right), (coup_hbm, coup),
        ))
    ]
    for load in loads:
        load.start()
    running[...] = jnp.zeros_like(running)

    barrier = pltpu.get_barrier_semaphore()
    for d in range(1, low):
        peer = hi * low + (lo + d) % low
        pl.semaphore_signal(barrier, inc=1, device_id={"row": peer}, device_id_type=MESH)
    for d in range(1, HIGH):
        peer = ((hi + d) % HIGH) * low + lo
        pl.semaphore_signal(barrier, inc=1, device_id={"row": peer}, device_id_type=MESH)

    @pl.when(sec > 0)
    def _():
        pl.semaphore_signal(
            barrier, inc=1, device_id={"section": sec - 1}, device_id_type=MESH
        )

    @pl.when(sec < sections - 1)
    def _():
        pl.semaphore_signal(
            barrier, inc=1, device_id={"section": sec + 1}, device_id_type=MESH
        )

    ends = jnp.where(sec > 0, 1, 0) + jnp.where(sec < sections - 1, 1, 0)
    pl.semaphore_wait(barrier, (low - 1) + (HIGH - 1) + ends)

    own = low - 1
    piece = rows // FIRST_PIECES

    def low_transfer(d, span, far, send_sem, recv_sem):
        return pltpu.make_async_remote_copy(
            src_ref=part.at[d - 1, span, far],
            dst_ref=got_low.at[d - 1, span, far],
            send_sem=send_sem,
            recv_sem=recv_sem,
            device_id={"row": hi * low + (lo + d) % low},
            device_id_type=MESH,
        )

    def first_copy(d, r):
        return low_transfer(d, pl.ds(r * piece, piece), 0, fs.at[d - 1, r], fr.at[d - 1, r])

    def low_copy(d, k):
        return low_transfer(d, k, pl.ds(1, HIGH - 1), ls.at[d - 1, k], lr.at[d - 1, k])

    def high_copy(d, k):
        return pltpu.make_async_remote_copy(
            src_ref=part.at[own, k, d - 1],
            dst_ref=got_high.at[d - 1, k],
            send_sem=hs.at[d - 1, k],
            recv_sem=hr.at[d - 1, k],
            device_id={"row": ((hi + d) % HIGH) * low + lo},
            device_id_type=MESH,
        )

    def merge(k, far):
        total = part[own, k, far].astype(jnp.float32)
        for d in range(1, low):
            total += got_low[d - 1, k, far].astype(jnp.float32)
        part[own, k, far] = total.astype(part.dtype)

    def chain_copy(k, target):
        return pltpu.make_async_remote_copy(
            src_ref=adj.at[k],
            dst_ref=later.at[k],
            send_sem=vs.at[k],
            recv_sem=vr.at[k],
            device_id={"section": target},
            device_id_type=MESH,
        )

    def products(at, pivots, order, first, second, run):
        scaled = [
            jnp.dot(
                first[index[order, j]], pinv[index[pivots, j]],
                preferred_element_type=jnp.float32,
            ).astype(jnp.bfloat16)
            for j in at
        ]
        updates = [
            jnp.dot(half, second[index[order, j]], preferred_element_type=jnp.float32)
            for half, j in zip(scaled, at)
        ]
        for update, j in zip(updates, at):
            same = index[order + 2, j] == index[order + 2, jnp.maximum(j - 1, 0)]
            run = run * jnp.where(same, 1.0, 0.0) + update
            sums[j] = run
        return run

    for load in loads[:3]:
        load.wait()

    def owner_group(q, run):
        far, near = q // low, q % low
        for p in range(CAP // GROUP):
            at = [q * CAP + p * GROUP + i for i in range(GROUP)]
            run = products(at, 6, 5, cleft, cright, run)
        for k in range(rows):
            spot = q * rows + k
            line, place = spot // LANES, spot % LANES
            used = jnp.where(index[12 + line, place] > 0, 1.0, 0.0)
            total = sums[jnp.maximum(index[8 + line, place], 0)] * used
            part[near, k, far] = total.astype(part.dtype)
        for d in range(1, low):

            @pl.when(q == d - 1)
            def _():
                for r in range(FIRST_PIECES):
                    first_copy(d, r).start()

        return run

    def owner_group_and_merge(q, run):
        run = owner_group(q, run)
        r = q - (HIGH * low - FIRST_PIECES)
        for d in range(1, low):
            first_copy(d, r).wait_recv()
        for i in range(piece):
            merge(r * piece + i, 0)
            high_copy(1, r * piece + i).start()
        return run

    plain = HIGH * low - FIRST_PIECES
    run = lax.fori_loop(0, plain, owner_group, jnp.zeros((width, width), jnp.float32))
    lax.fori_loop(plain, HIGH * low, owner_group_and_merge, run)

    for k in range(DEPTH):
        for d in range(1, low):
            low_copy(d, k).start()

    def new_write(k):
        return pltpu.make_async_copy(new.at[k], new_hbm.at[k], ns.at[k])

    def adj_write(k):
        return pltpu.make_async_copy(adj.at[k], adj_hbm.at[k], ads.at[k])

    def local_group(g, run):
        at = [g * GROUP + i for i in range(GROUP)]
        return products(at, 1, 0, left, right, run)

    def local_row(k, carry):
        used = jnp.where(index[4, k] > 0, 1.0, 0.0)
        total = sums[jnp.maximum(index[3, k], 0)] * used
        base[k] = coup[k].astype(jnp.float32) - total
        return carry

    def finish_row(j, carry):
        for d in range(1, HIGH):
            high_copy(d, j).wait_recv()
        total = part[own, j, HIGH - 1].astype(jnp.float32)
        for d in range(1, HIGH):
            total += got_high[d - 1, j].astype(jnp.float32)
        total = base[j] - total
        new[j] = total
        new_write(j).start()
        matrix_high[j], matrix_low[j] = split(
            three_products(split(diag[j]), split(total), ((1,), (0,)))
        )
        return carry

    def solve_row(m, carry):
        chain_copy(m, sec).wait_recv()
        adj[m] -= three_products(
            split(later[m]), (matrix_high[m], matrix_low[m]), ((1,), (1,))
        )

        @pl.when(sec > 0)
        def _():
            chain_copy(m, sec - 1).start()

        adj_write(m).start()
        return carry

    def finished(c):
        return jnp.where(c < LOCAL_STEPS, 0, jnp.clip(c - LAG + 1, 0, rows))


    def step(c, carry):
        @pl.when(c + DEPTH < rows)
        def _():
            for d in range(1, low):
                low_copy(d, c + DEPTH).start()

        @pl.when(c < rows)
        def _():
            for d in range(1, low):
                low_copy(d, c).wait_recv()
            for far in range(1, HIGH):
                merge(c, far)
                if far < HIGH - 1:
                    high_copy(far + 1, c).start()

        @pl.when(c == 0)
        def _():
            for load in loads[3:]:
                load.wait()

        @pl.when(c < rows)
        def _():
            adj[c] = three_products(split(seed[c]), split(diag[c]), ((1,), (1,)))

        @pl.when((c < rows) & (sec == sections - 1))
        def _():
            chain_copy(c, sec - 1).start()
            adj_write(c).start()

        @pl.when(c < LOCAL_STEPS)
        def _():
            per_step = slots // (LOCAL_STEPS * GROUP)
            running[...] = lax.fori_loop(
                c * per_step, (c + 1) * per_step, local_group, running[...]
            )

        @pl.when(c == LOCAL_STEPS - 1)
        def _():
            lax.fori_loop(0, rows, local_row, 0)

        lax.fori_loop(finished(c - 1), finished(c), finish_row, 0)
        delay = sections - 2 - sec

        @pl.when(sec < sections - 1)
        def _():
            lax.fori_loop(finished(c - 1 - delay), finished(c - delay), solve_row, 0)

        return carry

    lax.fori_loop(0, rows + LAG + sections - 2, step, 0)

    def drain(k, carry):
        new_write(k).wait()
        adj_write(k).wait()
        for d in range(1, low):
            low_copy(d, k).wait_send()
        for d in range(1, HIGH):
            high_copy(d, k).wait_send()

        @pl.when(sec > 0)
        def _():
            chain_copy(k, sec - 1).wait_send()

        return carry

    lax.fori_loop(0, rows, drain, 0)
    for r in range(FIRST_PIECES):
        for d in range(1, low):
            first_copy(d, r).wait_send()


def per_device(
    coupling,
    diag_inverse,
    pivot_inverse,
    cross_left,
    cross_right,
    cross_pivot,
    cross_owner,
    foreign_target_row,
    cross_count,
    local_left,
    local_right,
    local_pivot,
    local_target,
    adjoint_seed,
):
    rows, width, _ = coupling.shape
    groups = lax.axis_size("row")
    sections = lax.axis_size("section")
    low = groups // HIGH
    slots, local_slots = cross_left.shape[0], local_left.shape[0]
    block = (width, width)
    scalars = pl.BlockSpec(memory_space=pltpu.SMEM)
    vector = pl.BlockSpec(memory_space=pltpu.VMEM)

    def flat(x):
        return x.reshape(1, x.size)

    index = pl.pallas_call(
        functools.partial(order_kernel, low, rows),
        out_shape=jax.ShapeDtypeStruct((16, slots), jnp.int32),
        in_specs=[scalars] + [vector] * 5,
        out_specs=vector,
        name="order",
    )(cross_count, flat(cross_pivot), flat(cross_owner), flat(foreign_target_row),
      flat(local_pivot), flat(local_target))

    hbm = pl.BlockSpec(memory_space=pl.ANY)
    dma = pltpu.SemaphoreType.DMA
    outs = (
        jax.ShapeDtypeStruct((rows,) + block, jnp.float32),
        jax.ShapeDtypeStruct((rows,) + block, jnp.float32),
    )
    results = pl.pallas_call(
        functools.partial(exchange_kernel, low, sections),
        out_shape=outs,
        in_specs=[scalars] + [hbm] * 8,
        out_specs=(hbm, hbm),
        scratch_shapes=[
            pltpu.VMEM((low, rows, HIGH) + block, jnp.bfloat16),
            pltpu.VMEM((low - 1, rows, HIGH) + block, jnp.bfloat16),
            pltpu.VMEM((HIGH - 1, rows) + block, jnp.bfloat16),
            pltpu.VMEM((rows,) + block, jnp.float32),
            pltpu.VMEM((rows,) + block, jnp.bfloat16),
            pltpu.VMEM((rows,) + block, jnp.bfloat16),
            pltpu.VMEM((rows,) + block, jnp.float32),
            pltpu.VMEM((rows,) + block, jnp.float32),
            pltpu.VMEM((rows,) + block, jnp.float32),
            pltpu.VMEM(coupling.shape, coupling.dtype),
            pltpu.VMEM(diag_inverse.shape, jnp.float32),
            pltpu.VMEM(adjoint_seed.shape, jnp.float32),
            pltpu.VMEM(pivot_inverse.shape, pivot_inverse.dtype),
            pltpu.VMEM(cross_left.shape, cross_left.dtype),
            pltpu.VMEM(cross_right.shape, cross_right.dtype),
            pltpu.VMEM(local_left.shape, local_left.dtype),
            pltpu.VMEM(local_right.shape, local_right.dtype),
            pltpu.VMEM((local_slots,) + block, jnp.float32),
            pltpu.VMEM(block, jnp.float32),
            dma((8,)),
            dma((low - 1, FIRST_PIECES)),
            dma((low - 1, FIRST_PIECES)),
            dma((low - 1, rows)),
            dma((low - 1, rows)),
            dma((HIGH - 1, rows)),
            dma((HIGH - 1, rows)),
            dma((rows,)),
            dma((rows,)),
            dma((rows,)),
            dma((rows,)),
        ],
        compiler_params=pltpu.CompilerParams(
            collective_id=0, has_side_effects=True, vmem_limit_bytes=VMEM_LIMIT
        ),
        name="exchange",
    )(index, cross_left, cross_right, coupling, diag_inverse, adjoint_seed, pivot_inverse,
      local_left, local_right)
    return pl.pallas_call(
        results_kernel,
        out_shape=outs,
        in_specs=[hbm, hbm],
        out_specs=(hbm, hbm),
        scratch_shapes=[pltpu.VMEM((2, rows) + block, jnp.float32), dma((2, 4)), dma((2, 4))],
        compiler_params=pltpu.CompilerParams(vmem_limit_bytes=VMEM_LIMIT),
        name="results",
    )(*results)


def solution(mesh):
    spread = P(("section", "row"))
    return jax.shard_map(
        per_device,
        mesh=mesh,
        in_specs=(spread,) * 14,
        out_specs=(spread, spread),
        check_vma=False,
    )
```

```python
import functools

import jax
import jax.numpy as jnp
from jax import lax
from jax.experimental import pallas as pl
from jax.experimental.pallas import tpu as pltpu
from jax.sharding import PartitionSpec as P

GROUP = 8
DEPTH = 4
HIGH = 4
LAG = 3
LOCAL_STEPS = 4
CAP = 16
FIRST_PIECES = 4
LANES = 128
VMEM_LIMIT = 56 * 1024 * 1024
MESH = pl.DeviceIdType.MESH


def order_kernel(low, rows, ccount, cpiv, cown, crow, lpiv, lrow, index):
    n = cpiv.shape[1]
    row = lax.axis_index("row")
    hi, lo = row // low, row % low
    lane = lax.broadcasted_iota(jnp.int32, (n, n), 1).astype(jnp.float32)
    slot = lax.broadcasted_iota(jnp.int32, (n, n), 0).astype(jnp.float32)

    def down(x):
        return jnp.broadcast_to(x, (n, n)).T

    def total(x):
        return jnp.sum(x, axis=0, keepdims=True)

    def put(at, x):
        index[at:at + 1, :] = x.astype(jnp.int32)

    def sort(at, key, pivot):
        key_down = down(key)
        spread = key * n + lane[:1]
        rank = total(jnp.where(down(spread) < spread, 1.0, 0.0))
        hit = down(rank) == lane
        put(at, total(jnp.where(hit, slot, 0.0)))
        put(at + 1, total(jnp.where(hit, down(pivot), 0.0)))
        put(at + 2, total(jnp.where(hit, key_down, 0.0)))
        return key_down

    def ends(at, at_count, key_down, first):
        put(at, total(jnp.where(key_down <= lane + first, 1.0, 0.0)) - 1.0)
        put(at_count, total(jnp.where(key_down == lane + first, 1.0, 0.0)))

    local_down = sort(0, lrow[...].astype(jnp.float32), lpiv[...].astype(jnp.float32))
    ends(3, 4, local_down, 0.0)
    owner = cown[...]
    far = ((owner // low) - hi - 1) & (HIGH - 1)
    near = ((owner & (low - 1)) - lo - 1) & (low - 1)
    key = (far * low + near) * rows + crow[...]
    slot_number = lax.broadcasted_iota(jnp.int32, (1, n), 1)
    targets = HIGH * low * rows
    key = jnp.where(slot_number < ccount[0], key, targets)
    cross_down = sort(5, key.astype(jnp.float32), cpiv[...].astype(jnp.float32))
    for p in range(targets // n):
        ends(8 + p, 12 + p, cross_down, float(p * n))


def results_kernel(new_in, adj_in, new_out, adj_out, held, in_sems, out_sems):
    pieces = in_sems.shape[1]
    size = new_in.shape[0] // pieces
    reads, writes = [], []
    for a, (source, target) in enumerate(((new_in, new_out), (adj_in, adj_out))):
        for p in range(pieces):
            span = pl.ds(p * size, size)
            reads.append(
                pltpu.make_async_copy(source.at[span], held.at[a, span], in_sems.at[a, p])
            )
            writes.append(
                pltpu.make_async_copy(held.at[a, span], target.at[span], out_sems.at[a, p])
            )
    for read in reads:
        read.start()
    for read, write in zip(reads, writes):
        read.wait()
        write.start()
    for write in writes:
        write.wait()


def split(x):
    high = x.astype(jnp.bfloat16)
    return high, (x - high.astype(jnp.float32)).astype(jnp.bfloat16)


def three_products(left, right, contract):
    def one(a, b):
        return lax.dot_general(a, b, (contract, ((), ())), preferred_element_type=jnp.float32)

    return one(left[0], right[0]) + (one(left[0], right[1]) + one(left[1], right[0]))


def exchange_kernel(
    low, sections, index, cleft_hbm, cright_hbm, coup_hbm, diag_hbm, seed_hbm, pinv_hbm,
    left_hbm, right_hbm,
    new_hbm, adj_hbm,
    part, got_low, got_high, relayed, later, matrix_high, matrix_low, new, adj,
    base, coup, diag, seed, pinv, cleft, cright, left, right, sums, running,
    load_sem, fs, fr, ls, lr, hs, hr, rs, rr, vs, vr, ns, ads,
):
    rows, width, _ = base.shape
    slots = left.shape[0]
    row = lax.axis_index("row")
    sec = lax.axis_index("section")
    hi, lo = row // low, row % low

    loads = [
        pltpu.make_async_copy(source, target, load_sem.at[i])
        for i, (source, target) in enumerate((
            (pinv_hbm, pinv), (cleft_hbm, cleft), (cright_hbm, cright), (seed_hbm, seed),
            (diag_hbm, diag), (left_hbm, left), (right_hbm, right), (coup_hbm, coup),
        ))
    ]
    for load in loads:
        load.start()
    running[...] = jnp.zeros_like(running)

    @pl.when(hi == 0)
    def _():
        got_high[0] = jnp.zeros(got_high.shape[1:], got_high.dtype)

    @pl.when(hi == HIGH - 1)
    def _():
        got_high[HIGH - 2] = jnp.zeros(got_high.shape[1:], got_high.dtype)


    barrier = pltpu.get_barrier_semaphore()
    for d in range(1, low):
        peer = hi * low + (lo + d) % low
        pl.semaphore_signal(barrier, inc=1, device_id={"row": peer}, device_id_type=MESH)
    for d in range(1, HIGH):
        peer = ((hi + d) % HIGH) * low + lo
        pl.semaphore_signal(barrier, inc=1, device_id={"row": peer}, device_id_type=MESH)

    @pl.when(sec > 0)
    def _():
        pl.semaphore_signal(
            barrier, inc=1, device_id={"section": sec - 1}, device_id_type=MESH
        )

    @pl.when(sec < sections - 1)
    def _():
        pl.semaphore_signal(
            barrier, inc=1, device_id={"section": sec + 1}, device_id_type=MESH
        )

    ends = jnp.where(sec > 0, 1, 0) + jnp.where(sec < sections - 1, 1, 0)
    pl.semaphore_wait(barrier, (low - 1) + (HIGH - 1) + ends)

    own = low - 1
    piece = rows // FIRST_PIECES

    def low_transfer(d, span, far, send_sem, recv_sem):
        return pltpu.make_async_remote_copy(
            src_ref=part.at[d - 1, span, far],
            dst_ref=got_low.at[d - 1, span, far],
            send_sem=send_sem,
            recv_sem=recv_sem,
            device_id={"row": hi * low + (lo + d) % low},
            device_id_type=MESH,
        )

    def first_copy(d, r):
        return low_transfer(d, pl.ds(r * piece, piece), 0, fs.at[d - 1, r], fr.at[d - 1, r])

    def low_copy(d, k):
        return low_transfer(d, k, pl.ds(1, HIGH - 1), ls.at[d - 1, k], lr.at[d - 1, k])

    def high_copy(d, k):
        return pltpu.make_async_remote_copy(
            src_ref=part.at[own, k, d - 1],
            dst_ref=got_high.at[d - 1, k],
            send_sem=hs.at[d - 1, k],
            recv_sem=hr.at[d - 1, k],
            device_id={"row": ((hi + d) % HIGH) * low + lo},
            device_id_type=MESH,
        )

    edge = (hi == 0) | (hi == HIGH - 1)

    def relay_copy(k):
        return pltpu.make_async_remote_copy(
            src_ref=part.at[own, k, jnp.where(hi == 0, HIGH - 2, 0)],
            dst_ref=relayed.at[k],
            send_sem=rs.at[k],
            recv_sem=rr.at[k],
            device_id={"row": jnp.where(hi == 0, 1, HIGH - 2) * low + lo},
            device_id_type=MESH,
        )

    def sends_far(d):
        return {1: hi == HIGH - 1, HIGH - 1: hi == 0}.get(d)

    def gets_none(d):
        return {1: hi == 0, HIGH - 1: hi == HIGH - 1}.get(d)

    def unless(condition, act):
        if condition is None:
            act()
        else:
            pl.when(jnp.logical_not(condition))(act)

    def send_high(d, k):
        unless(sends_far(d), lambda: high_copy(d, k).start())
        if sends_far(d) is not None:
            pl.when(sends_far(d))(lambda: relay_copy(k).start())

    def send_middle(k):
        @pl.when(jnp.logical_not(edge))
        def _():
            relay_copy(k).wait_recv()
            total = part[own, k, 1].astype(jnp.float32) + relayed[k].astype(jnp.float32)
            part[own, k, 1] = total.astype(part.dtype)

        send_high(2, k)

    def merge(k, far):
        total = part[own, k, far].astype(jnp.float32)
        for d in range(1, low):
            total += got_low[d - 1, k, far].astype(jnp.float32)
        part[own, k, far] = total.astype(part.dtype)

    def chain_copy(k, target):
        return pltpu.make_async_remote_copy(
            src_ref=adj.at[k],
            dst_ref=later.at[k],
            send_sem=vs.at[k],
            recv_sem=vr.at[k],
            device_id={"section": target},
            device_id_type=MESH,
        )

    def products(at, pivots, order, first, second, run):
        scaled = [
            jnp.dot(
                first[index[order, j]], pinv[index[pivots, j]],
                preferred_element_type=jnp.float32,
            ).astype(jnp.bfloat16)
            for j in at
        ]
        updates = [
            jnp.dot(half, second[index[order, j]], preferred_element_type=jnp.float32)
            for half, j in zip(scaled, at)
        ]
        for update, j in zip(updates, at):
            same = index[order + 2, j] == index[order + 2, jnp.maximum(j - 1, 0)]
            run = run * jnp.where(same, 1.0, 0.0) + update
            sums[j] = run
        return run

    for load in loads[:3]:
        load.wait()

    def owner_group(q, run):
        far, near = q // low, q % low
        for p in range(CAP // GROUP):
            at = [q * CAP + p * GROUP + i for i in range(GROUP)]
            run = products(at, 6, 5, cleft, cright, run)
        for k in range(rows):
            spot = q * rows + k
            line, place = spot // LANES, spot % LANES
            used = jnp.where(index[12 + line, place] > 0, 1.0, 0.0)
            total = sums[jnp.maximum(index[8 + line, place], 0)] * used
            part[near, k, far] = total.astype(part.dtype)
        for d in range(1, low):

            @pl.when(q == d - 1)
            def _():
                for r in range(FIRST_PIECES):
                    first_copy(d, r).start()

        return run

    def owner_group_and_merge(q, run):
        run = owner_group(q, run)
        r = q - (HIGH * low - FIRST_PIECES)
        for d in range(1, low):
            first_copy(d, r).wait_recv()
        for i in range(piece):
            merge(r * piece + i, 0)
            send_high(1, r * piece + i)
        return run

    plain = HIGH * low - FIRST_PIECES
    run = lax.fori_loop(0, plain, owner_group, jnp.zeros((width, width), jnp.float32))
    lax.fori_loop(plain, HIGH * low, owner_group_and_merge, run)

    for k in range(DEPTH):
        for d in range(1, low):
            low_copy(d, k).start()

    def new_write(k):
        return pltpu.make_async_copy(new.at[k], new_hbm.at[k], ns.at[k])

    def adj_write(k):
        return pltpu.make_async_copy(adj.at[k], adj_hbm.at[k], ads.at[k])

    def local_group(g, run):
        at = [g * GROUP + i for i in range(GROUP)]
        return products(at, 1, 0, left, right, run)

    def local_row(k, carry):
        used = jnp.where(index[4, k] > 0, 1.0, 0.0)
        total = sums[jnp.maximum(index[3, k], 0)] * used
        base[k] = coup[k].astype(jnp.float32) - total
        return carry

    def finish_row(j, carry):
        for d in range(1, HIGH):
            unless(gets_none(d), lambda d=d: high_copy(d, j).wait_recv())
        total = part[own, j, HIGH - 1].astype(jnp.float32)
        for d in range(1, HIGH):
            total += got_high[d - 1, j].astype(jnp.float32)
        total = base[j] - total
        new[j] = total
        new_write(j).start()
        matrix_high[j], matrix_low[j] = split(
            three_products(split(diag[j]), split(total), ((1,), (0,)))
        )
        return carry

    def solve_row(m, carry):
        chain_copy(m, sec).wait_recv()
        adj[m] -= three_products(
            split(later[m]), (matrix_high[m], matrix_low[m]), ((1,), (1,))
        )

        @pl.when(sec > 0)
        def _():
            chain_copy(m, sec - 1).start()

        adj_write(m).start()
        return carry

    def finished(c):
        return jnp.where(c < LOCAL_STEPS, 0, jnp.clip(c - LAG + 1, 0, rows))


    def step(c, carry):
        @pl.when(c + DEPTH < rows)
        def _():
            for d in range(1, low):
                low_copy(d, c + DEPTH).start()

        @pl.when(c < rows)
        def _():
            for d in range(1, low):
                low_copy(d, c).wait_recv()
            for far in range(1, HIGH):
                merge(c, far)
                if far == HIGH - 2:
                    send_high(HIGH - 1, c)

        @pl.when((c >= 1) & (c <= rows))
        def _():
            send_middle(c - 1)

        @pl.when(c == 0)
        def _():
            for load in loads[3:]:
                load.wait()

        @pl.when(c < rows)
        def _():
            adj[c] = three_products(split(seed[c]), split(diag[c]), ((1,), (1,)))

        @pl.when((c < rows) & (sec == sections - 1))
        def _():
            chain_copy(c, sec - 1).start()
            adj_write(c).start()

        @pl.when(c < LOCAL_STEPS)
        def _():
            per_step = slots // (LOCAL_STEPS * GROUP)
            running[...] = lax.fori_loop(
                c * per_step, (c + 1) * per_step, local_group, running[...]
            )

        @pl.when(c == LOCAL_STEPS - 1)
        def _():
            lax.fori_loop(0, rows, local_row, 0)

        lax.fori_loop(finished(c - 1), finished(c), finish_row, 0)
        delay = sections - 2 - sec

        @pl.when(sec < sections - 1)
        def _():
            lax.fori_loop(finished(c - 1 - delay), finished(c - delay), solve_row, 0)

        return carry

    lax.fori_loop(0, rows + LAG + sections - 2, step, 0)

    def drain(k, carry):
        new_write(k).wait()
        adj_write(k).wait()
        for d in range(1, low):
            low_copy(d, k).wait_send()
        for d in range(1, HIGH):
            unless(sends_far(d), lambda d=d: high_copy(d, k).wait_send())

        @pl.when(edge)
        def _():
            relay_copy(k).wait_send()

        @pl.when(sec > 0)
        def _():
            chain_copy(k, sec - 1).wait_send()

        return carry

    lax.fori_loop(0, rows, drain, 0)
    for r in range(FIRST_PIECES):
        for d in range(1, low):
            first_copy(d, r).wait_send()


def per_device(
    coupling,
    diag_inverse,
    pivot_inverse,
    cross_left,
    cross_right,
    cross_pivot,
    cross_owner,
    foreign_target_row,
    cross_count,
    local_left,
    local_right,
    local_pivot,
    local_target,
    adjoint_seed,
):
    rows, width, _ = coupling.shape
    groups = lax.axis_size("row")
    sections = lax.axis_size("section")
    low = groups // HIGH
    slots, local_slots = cross_left.shape[0], local_left.shape[0]
    block = (width, width)
    scalars = pl.BlockSpec(memory_space=pltpu.SMEM)
    vector = pl.BlockSpec(memory_space=pltpu.VMEM)

    def flat(x):
        return x.reshape(1, x.size)

    index = pl.pallas_call(
        functools.partial(order_kernel, low, rows),
        out_shape=jax.ShapeDtypeStruct((16, slots), jnp.int32),
        in_specs=[scalars] + [vector] * 5,
        out_specs=vector,
        name="order",
    )(cross_count, flat(cross_pivot), flat(cross_owner), flat(foreign_target_row),
      flat(local_pivot), flat(local_target))

    hbm = pl.BlockSpec(memory_space=pl.ANY)
    dma = pltpu.SemaphoreType.DMA
    outs = (
        jax.ShapeDtypeStruct((rows,) + block, jnp.float32),
        jax.ShapeDtypeStruct((rows,) + block, jnp.float32),
    )
    results = pl.pallas_call(
        functools.partial(exchange_kernel, low, sections),
        out_shape=outs,
        in_specs=[scalars] + [hbm] * 8,
        out_specs=(hbm, hbm),
        scratch_shapes=[
            pltpu.VMEM((low, rows, HIGH) + block, jnp.bfloat16),
            pltpu.VMEM((low - 1, rows, HIGH) + block, jnp.bfloat16),
            pltpu.VMEM((HIGH - 1, rows) + block, jnp.bfloat16),
            pltpu.VMEM((rows,) + block, jnp.bfloat16),
            pltpu.VMEM((rows,) + block, jnp.float32),
            pltpu.VMEM((rows,) + block, jnp.bfloat16),
            pltpu.VMEM((rows,) + block, jnp.bfloat16),
            pltpu.VMEM((rows,) + block, jnp.float32),
            pltpu.VMEM((rows,) + block, jnp.float32),
            pltpu.VMEM((rows,) + block, jnp.float32),
            pltpu.VMEM(coupling.shape, coupling.dtype),
            pltpu.VMEM(diag_inverse.shape, jnp.float32),
            pltpu.VMEM(adjoint_seed.shape, jnp.float32),
            pltpu.VMEM(pivot_inverse.shape, pivot_inverse.dtype),
            pltpu.VMEM(cross_left.shape, cross_left.dtype),
            pltpu.VMEM(cross_right.shape, cross_right.dtype),
            pltpu.VMEM(local_left.shape, local_left.dtype),
            pltpu.VMEM(local_right.shape, local_right.dtype),
            pltpu.VMEM((local_slots,) + block, jnp.float32),
            pltpu.VMEM(block, jnp.float32),
            dma((8,)),
            dma((low - 1, FIRST_PIECES)),
            dma((low - 1, FIRST_PIECES)),
            dma((low - 1, rows)),
            dma((low - 1, rows)),
            dma((HIGH - 1, rows)),
            dma((HIGH - 1, rows)),
            dma((rows,)),
            dma((rows,)),
            dma((rows,)),
            dma((rows,)),
            dma((rows,)),
            dma((rows,)),
        ],
        compiler_params=pltpu.CompilerParams(
            collective_id=0, has_side_effects=True, vmem_limit_bytes=VMEM_LIMIT
        ),
        name="exchange",
    )(index, cross_left, cross_right, coupling, diag_inverse, adjoint_seed, pivot_inverse,
      local_left, local_right)
    return pl.pallas_call(
        results_kernel,
        out_shape=outs,
        in_specs=[hbm, hbm],
        out_specs=(hbm, hbm),
        scratch_shapes=[pltpu.VMEM((2, rows) + block, jnp.float32), dma((2, 4)), dma((2, 4))],
        compiler_params=pltpu.CompilerParams(vmem_limit_bytes=VMEM_LIMIT),
        name="results",
    )(*results)


def solution(mesh):
    spread = P(("section", "row"))
    return jax.shard_map(
        per_device,
        mesh=mesh,
        in_specs=(spread,) * 14,
        out_specs=(spread, spread),
        check_vma=False,
    )
```

```python
import functools

import jax
import jax.numpy as jnp
from jax import lax
from jax.experimental import pallas as pl
from jax.experimental.pallas import tpu as pltpu
from jax.sharding import PartitionSpec as P

GROUP = 8
DEPTH = 4
HIGH = 4
LAG = 3
LOCAL_STEPS = 4
CAP = 16
FIRST_PIECES = 4
LANES = 128
VMEM_LIMIT = 56 * 1024 * 1024
MESH = pl.DeviceIdType.MESH


def order_kernel(low, rows, ccount, cpiv, cown, crow, lpiv, lrow, index):
    n = cpiv.shape[1]
    row = lax.axis_index("row")
    hi, lo = row // low, row % low
    lane = lax.broadcasted_iota(jnp.int32, (n, n), 1).astype(jnp.float32)
    slot = lax.broadcasted_iota(jnp.int32, (n, n), 0).astype(jnp.float32)

    def down(x):
        return jnp.broadcast_to(x, (n, n)).T

    def total(x):
        return jnp.sum(x, axis=0, keepdims=True)

    def put(at, x):
        index[at:at + 1, :] = x.astype(jnp.int32)

    def sort(at, key, pivot):
        key_down = down(key)
        spread = key * n + lane[:1]
        rank = total(jnp.where(down(spread) < spread, 1.0, 0.0))
        hit = down(rank) == lane
        put(at, total(jnp.where(hit, slot, 0.0)))
        put(at + 1, total(jnp.where(hit, down(pivot), 0.0)))
        put(at + 2, total(jnp.where(hit, key_down, 0.0)))
        return key_down

    def ends(at, at_count, key_down, first):
        put(at, total(jnp.where(key_down <= lane + first, 1.0, 0.0)) - 1.0)
        put(at_count, total(jnp.where(key_down == lane + first, 1.0, 0.0)))

    local_down = sort(0, lrow[...].astype(jnp.float32), lpiv[...].astype(jnp.float32))
    ends(3, 4, local_down, 0.0)
    owner = cown[...]
    far = ((owner // low) - hi - 1) & (HIGH - 1)
    near = ((owner & (low - 1)) - lo - 1) & (low - 1)
    key = (near * HIGH + far) * rows + crow[...]
    slot_number = lax.broadcasted_iota(jnp.int32, (1, n), 1)
    targets = HIGH * low * rows
    key = jnp.where(slot_number < ccount[0], key, targets)
    cross_down = sort(5, key.astype(jnp.float32), cpiv[...].astype(jnp.float32))
    for p in range(targets // n):
        ends(8 + p, 12 + p, cross_down, float(p * n))


def results_kernel(new_in, adj_in, new_out, adj_out, held, in_sems, out_sems):
    pieces = in_sems.shape[1]
    size = new_in.shape[0] // pieces
    reads, writes = [], []
    for a, (source, target) in enumerate(((new_in, new_out), (adj_in, adj_out))):
        for p in range(pieces):
            span = pl.ds(p * size, size)
            reads.append(
                pltpu.make_async_copy(source.at[span], held.at[a, span], in_sems.at[a, p])
            )
            writes.append(
                pltpu.make_async_copy(held.at[a, span], target.at[span], out_sems.at[a, p])
            )
    for read in reads:
        read.start()
    for read, write in zip(reads, writes):
        read.wait()
        write.start()
    for write in writes:
        write.wait()


def split(x):
    high = x.astype(jnp.bfloat16)
    return high, (x - high.astype(jnp.float32)).astype(jnp.bfloat16)


def three_products(left, right, contract):
    def one(a, b):
        return lax.dot_general(a, b, (contract, ((), ())), preferred_element_type=jnp.float32)

    return one(left[0], right[0]) + (one(left[0], right[1]) + one(left[1], right[0]))


def exchange_kernel(
    low, sections, index, cleft_hbm, cright_hbm, coup_hbm, diag_hbm, seed_hbm, pinv_hbm,
    left_hbm, right_hbm,
    new_hbm, adj_hbm,
    part, got_low, got_high, relayed, later, matrix_high, matrix_low, new, adj,
    base, coup, diag, seed, pinv, cleft, cright, left, right, sums, running,
    load_sem, fs, fr, ls, lr, hs, hr, rs, rr, vs, vr, ns, ads,
):
    rows, width, _ = base.shape
    slots = left.shape[0]
    row = lax.axis_index("row")
    sec = lax.axis_index("section")
    hi, lo = row // low, row % low

    loads = [
        pltpu.make_async_copy(source, target, load_sem.at[i])
        for i, (source, target) in enumerate((
            (pinv_hbm, pinv), (cleft_hbm, cleft), (cright_hbm, cright), (seed_hbm, seed),
            (diag_hbm, diag), (left_hbm, left), (right_hbm, right), (coup_hbm, coup),
        ))
    ]
    for load in loads:
        load.start()
    running[...] = jnp.zeros_like(running)

    @pl.when(hi == 0)
    def _():
        got_high[0] = jnp.zeros(got_high.shape[1:], got_high.dtype)

    @pl.when(hi == HIGH - 1)
    def _():
        got_high[HIGH - 2] = jnp.zeros(got_high.shape[1:], got_high.dtype)


    barrier = pltpu.get_barrier_semaphore()
    for d in range(1, low):
        peer = hi * low + (lo + d) % low
        pl.semaphore_signal(barrier, inc=1, device_id={"row": peer}, device_id_type=MESH)
    for d in range(1, HIGH):
        peer = ((hi + d) % HIGH) * low + lo
        pl.semaphore_signal(barrier, inc=1, device_id={"row": peer}, device_id_type=MESH)

    @pl.when(sec > 0)
    def _():
        pl.semaphore_signal(
            barrier, inc=1, device_id={"section": sec - 1}, device_id_type=MESH
        )

    @pl.when(sec < sections - 1)
    def _():
        pl.semaphore_signal(
            barrier, inc=1, device_id={"section": sec + 1}, device_id_type=MESH
        )

    ends = jnp.where(sec > 0, 1, 0) + jnp.where(sec < sections - 1, 1, 0)
    pl.semaphore_wait(barrier, (low - 1) + (HIGH - 1) + ends)

    own = low - 1
    piece = rows // FIRST_PIECES

    def low_transfer(d, span, far, send_sem, recv_sem):
        return pltpu.make_async_remote_copy(
            src_ref=part.at[d - 1, span, far],
            dst_ref=got_low.at[d - 1, span, far],
            send_sem=send_sem,
            recv_sem=recv_sem,
            device_id={"row": hi * low + (lo + d) % low},
            device_id_type=MESH,
        )

    def first_copy(d, r):
        return low_transfer(d, pl.ds(r * piece, piece), 0, fs.at[d - 1, r], fr.at[d - 1, r])

    def low_copy(d, k):
        return low_transfer(d, k, pl.ds(1, HIGH - 1), ls.at[d - 1, k], lr.at[d - 1, k])

    def high_copy(d, k):
        return pltpu.make_async_remote_copy(
            src_ref=part.at[own, k, d - 1],
            dst_ref=got_high.at[d - 1, k],
            send_sem=hs.at[d - 1, k],
            recv_sem=hr.at[d - 1, k],
            device_id={"row": ((hi + d) % HIGH) * low + lo},
            device_id_type=MESH,
        )

    edge = (hi == 0) | (hi == HIGH - 1)

    def relay_copy(k):
        return pltpu.make_async_remote_copy(
            src_ref=part.at[own, k, jnp.where(hi == 0, HIGH - 2, 0)],
            dst_ref=relayed.at[k],
            send_sem=rs.at[k],
            recv_sem=rr.at[k],
            device_id={"row": jnp.where(hi == 0, 1, HIGH - 2) * low + lo},
            device_id_type=MESH,
        )

    def sends_far(d):
        return {1: hi == HIGH - 1, HIGH - 1: hi == 0}.get(d)

    def gets_none(d):
        return {1: hi == 0, HIGH - 1: hi == HIGH - 1}.get(d)

    def unless(condition, act):
        if condition is None:
            act()
        else:
            pl.when(jnp.logical_not(condition))(act)

    def send_high(d, k):
        unless(sends_far(d), lambda: high_copy(d, k).start())
        if sends_far(d) is not None:
            pl.when(sends_far(d))(lambda: relay_copy(k).start())

    def send_middle(k):
        @pl.when(jnp.logical_not(edge))
        def _():
            relay_copy(k).wait_recv()
            total = part[own, k, 1].astype(jnp.float32) + relayed[k].astype(jnp.float32)
            part[own, k, 1] = total.astype(part.dtype)

        send_high(2, k)

    def merge(k, far):
        total = part[own, k, far].astype(jnp.float32)
        for d in range(1, low):
            total += got_low[d - 1, k, far].astype(jnp.float32)
        part[own, k, far] = total.astype(part.dtype)

    def chain_copy(k, target):
        return pltpu.make_async_remote_copy(
            src_ref=adj.at[k],
            dst_ref=later.at[k],
            send_sem=vs.at[k],
            recv_sem=vr.at[k],
            device_id={"section": target},
            device_id_type=MESH,
        )

    def products(at, pivots, order, first, second, run):
        scaled = [
            jnp.dot(
                first[index[order, j]], pinv[index[pivots, j]],
                preferred_element_type=jnp.float32,
            ).astype(jnp.bfloat16)
            for j in at
        ]
        updates = [
            jnp.dot(half, second[index[order, j]], preferred_element_type=jnp.float32)
            for half, j in zip(scaled, at)
        ]
        for update, j in zip(updates, at):
            same = index[order + 2, j] == index[order + 2, jnp.maximum(j - 1, 0)]
            run = run * jnp.where(same, 1.0, 0.0) + update
            sums[j] = run
        return run

    for load in loads[:3]:
        load.wait()

    def owner_group(q, run):
        far, near = q % HIGH, q // HIGH
        for p in range(CAP // GROUP):
            at = [q * CAP + p * GROUP + i for i in range(GROUP)]
            run = products(at, 6, 5, cleft, cright, run)
        for k in range(rows):
            spot = q * rows + k
            line, place = spot // LANES, spot % LANES
            used = jnp.where(index[12 + line, place] > 0, 1.0, 0.0)
            total = sums[jnp.maximum(index[8 + line, place], 0)] * used
            part[near, k, far] = total.astype(part.dtype)
        for d in range(1, low):

            @pl.when(q == (d - 1) * HIGH)
            def _():
                for r in range(FIRST_PIECES):
                    first_copy(d, r).start()

        @pl.when(q == own * HIGH - 1)
        def _():
            for k in range(DEPTH):
                for d in range(1, low):
                    low_copy(d, k).start()

        return run

    def owner_group_and_merge(q, run):
        run = owner_group(q, run)
        r = q - (HIGH * low - FIRST_PIECES)
        for d in range(1, low):
            first_copy(d, r).wait_recv()
        for i in range(piece):
            merge(r * piece + i, 0)
            send_high(1, r * piece + i)
        return run

    plain = HIGH * low - FIRST_PIECES
    run = lax.fori_loop(0, plain, owner_group, jnp.zeros((width, width), jnp.float32))
    lax.fori_loop(plain, HIGH * low, owner_group_and_merge, run)

    def new_write(k):
        return pltpu.make_async_copy(new.at[k], new_hbm.at[k], ns.at[k])

    def adj_write(k):
        return pltpu.make_async_copy(adj.at[k], adj_hbm.at[k], ads.at[k])

    def local_group(g, run):
        at = [g * GROUP + i for i in range(GROUP)]
        return products(at, 1, 0, left, right, run)

    def local_row(k, carry):
        used = jnp.where(index[4, k] > 0, 1.0, 0.0)
        total = sums[jnp.maximum(index[3, k], 0)] * used
        base[k] = coup[k].astype(jnp.float32) - total
        return carry

    def finish_row(j, carry):
        for d in range(1, HIGH):
            unless(gets_none(d), lambda d=d: high_copy(d, j).wait_recv())
        total = part[own, j, HIGH - 1].astype(jnp.float32)
        for d in range(1, HIGH):
            total += got_high[d - 1, j].astype(jnp.float32)
        total = base[j] - total
        new[j] = total
        new_write(j).start()
        matrix_high[j], matrix_low[j] = split(
            three_products(split(diag[j]), split(total), ((1,), (0,)))
        )
        return carry

    def solve_row(m, carry):
        chain_copy(m, sec).wait_recv()
        adj[m] -= three_products(
            split(later[m]), (matrix_high[m], matrix_low[m]), ((1,), (1,))
        )

        @pl.when(sec > 0)
        def _():
            chain_copy(m, sec - 1).start()

        adj_write(m).start()
        return carry

    def finished(c):
        done = jnp.where(c < rows, jnp.clip(c - LAG + 1, 0, rows), rows)
        return jnp.where(c < LOCAL_STEPS, 0, done)


    def step(c, carry):
        @pl.when(c + DEPTH < rows)
        def _():
            for d in range(1, low):
                low_copy(d, c + DEPTH).start()

        @pl.when(c < rows)
        def _():
            for d in range(1, low):
                low_copy(d, c).wait_recv()
            for far in range(1, HIGH):
                merge(c, far)
                if far == HIGH - 2:
                    send_high(HIGH - 1, c)

        @pl.when((c >= 1) & (c <= rows))
        def _():
            send_middle(c - 1)

        @pl.when(c == 0)
        def _():
            for load in loads[3:]:
                load.wait()

        @pl.when(c < rows)
        def _():
            adj[c] = three_products(split(seed[c]), split(diag[c]), ((1,), (1,)))

        @pl.when((c < rows) & (sec == sections - 1))
        def _():
            chain_copy(c, sec - 1).start()
            adj_write(c).start()

        @pl.when(c < LOCAL_STEPS)
        def _():
            per_step = slots // (LOCAL_STEPS * GROUP)
            running[...] = lax.fori_loop(
                c * per_step, (c + 1) * per_step, local_group, running[...]
            )

        @pl.when(c == LOCAL_STEPS - 1)
        def _():
            lax.fori_loop(0, rows, local_row, 0)

        lax.fori_loop(finished(c - 1), finished(c), finish_row, 0)
        delay = sections - 2 - sec

        @pl.when(sec < sections - 1)
        def _():
            lax.fori_loop(finished(c - 1 - delay), finished(c - delay), solve_row, 0)

        return carry

    lax.fori_loop(0, rows + sections - 1, step, 0)

    def drain(k, carry):
        new_write(k).wait()
        adj_write(k).wait()
        for d in range(1, low):
            low_copy(d, k).wait_send()
        for d in range(1, HIGH):
            unless(sends_far(d), lambda d=d: high_copy(d, k).wait_send())

        @pl.when(edge)
        def _():
            relay_copy(k).wait_send()

        @pl.when(sec > 0)
        def _():
            chain_copy(k, sec - 1).wait_send()

        return carry

    lax.fori_loop(0, rows, drain, 0)
    for r in range(FIRST_PIECES):
        for d in range(1, low):
            first_copy(d, r).wait_send()


def per_device(
    coupling,
    diag_inverse,
    pivot_inverse,
    cross_left,
    cross_right,
    cross_pivot,
    cross_owner,
    foreign_target_row,
    cross_count,
    local_left,
    local_right,
    local_pivot,
    local_target,
    adjoint_seed,
):
    rows, width, _ = coupling.shape
    groups = lax.axis_size("row")
    sections = lax.axis_size("section")
    low = groups // HIGH
    slots, local_slots = cross_left.shape[0], local_left.shape[0]
    block = (width, width)
    scalars = pl.BlockSpec(memory_space=pltpu.SMEM)
    vector = pl.BlockSpec(memory_space=pltpu.VMEM)

    def flat(x):
        return x.reshape(1, x.size)

    index = pl.pallas_call(
        functools.partial(order_kernel, low, rows),
        out_shape=jax.ShapeDtypeStruct((16, slots), jnp.int32),
        in_specs=[scalars] + [vector] * 5,
        out_specs=vector,
        name="order",
    )(cross_count, flat(cross_pivot), flat(cross_owner), flat(foreign_target_row),
      flat(local_pivot), flat(local_target))

    hbm = pl.BlockSpec(memory_space=pl.ANY)
    dma = pltpu.SemaphoreType.DMA
    outs = (
        jax.ShapeDtypeStruct((rows,) + block, jnp.float32),
        jax.ShapeDtypeStruct((rows,) + block, jnp.float32),
    )
    results = pl.pallas_call(
        functools.partial(exchange_kernel, low, sections),
        out_shape=outs,
        in_specs=[scalars] + [hbm] * 8,
        out_specs=(hbm, hbm),
        scratch_shapes=[
            pltpu.VMEM((low, rows, HIGH) + block, jnp.bfloat16),
            pltpu.VMEM((low - 1, rows, HIGH) + block, jnp.bfloat16),
            pltpu.VMEM((HIGH - 1, rows) + block, jnp.bfloat16),
            pltpu.VMEM((rows,) + block, jnp.bfloat16),
            pltpu.VMEM((rows,) + block, jnp.float32),
            pltpu.VMEM((rows,) + block, jnp.bfloat16),
            pltpu.VMEM((rows,) + block, jnp.bfloat16),
            pltpu.VMEM((rows,) + block, jnp.float32),
            pltpu.VMEM((rows,) + block, jnp.float32),
            pltpu.VMEM((rows,) + block, jnp.float32),
            pltpu.VMEM(coupling.shape, coupling.dtype),
            pltpu.VMEM(diag_inverse.shape, jnp.float32),
            pltpu.VMEM(adjoint_seed.shape, jnp.float32),
            pltpu.VMEM(pivot_inverse.shape, pivot_inverse.dtype),
            pltpu.VMEM(cross_left.shape, cross_left.dtype),
            pltpu.VMEM(cross_right.shape, cross_right.dtype),
            pltpu.VMEM(local_left.shape, local_left.dtype),
            pltpu.VMEM(local_right.shape, local_right.dtype),
            pltpu.VMEM((local_slots,) + block, jnp.float32),
            pltpu.VMEM(block, jnp.float32),
            dma((8,)),
            dma((low - 1, FIRST_PIECES)),
            dma((low - 1, FIRST_PIECES)),
            dma((low - 1, rows)),
            dma((low - 1, rows)),
            dma((HIGH - 1, rows)),
            dma((HIGH - 1, rows)),
            dma((rows,)),
            dma((rows,)),
            dma((rows,)),
            dma((rows,)),
            dma((rows,)),
            dma((rows,)),
        ],
        compiler_params=pltpu.CompilerParams(
            collective_id=0, has_side_effects=True, vmem_limit_bytes=VMEM_LIMIT
        ),
        name="exchange",
    )(index, cross_left, cross_right, coupling, diag_inverse, adjoint_seed, pivot_inverse,
      local_left, local_right)
    return pl.pallas_call(
        results_kernel,
        out_shape=outs,
        in_specs=[hbm, hbm],
        out_specs=(hbm, hbm),
        scratch_shapes=[pltpu.VMEM((2, rows) + block, jnp.float32), dma((2, 4)), dma((2, 4))],
        compiler_params=pltpu.CompilerParams(vmem_limit_bytes=VMEM_LIMIT),
        name="results",
    )(*results)


def solution(mesh):
    spread = P(("section", "row"))
    return jax.shard_map(
        per_device,
        mesh=mesh,
        in_specs=(spread,) * 14,
        out_specs=(spread, spread),
        check_vma=False,
    )
```

```python
import functools

import jax
import jax.numpy as jnp
from jax import lax
from jax.experimental import pallas as pl
from jax.experimental.pallas import tpu as pltpu
from jax.sharding import PartitionSpec as P

GROUP = 8
DEPTH = 4
HIGH = 4
LAG = 3
LOCAL_STEPS = 8
CAP = 16
FIRST_PIECES = 4
LANES = 128
VMEM_LIMIT = 56 * 1024 * 1024
MESH = pl.DeviceIdType.MESH


def order_kernel(low, rows, ccount, cpiv, cown, crow, lpiv, lrow, index):
    n = cpiv.shape[1]
    row = lax.axis_index("row")
    hi, lo = row // low, row % low
    lane = lax.broadcasted_iota(jnp.int32, (n, n), 1).astype(jnp.float32)
    slot = lax.broadcasted_iota(jnp.int32, (n, n), 0).astype(jnp.float32)

    def down(x):
        return jnp.broadcast_to(x, (n, n)).T

    def total(x):
        return jnp.sum(x, axis=0, keepdims=True)

    def put(at, x):
        index[at:at + 1, :] = x.astype(jnp.int32)

    def sort(at, key, pivot):
        key_down = down(key)
        spread = key * n + lane[:1]
        rank = total(jnp.where(down(spread) < spread, 1.0, 0.0))
        hit = down(rank) == lane
        put(at, total(jnp.where(hit, slot, 0.0)))
        put(at + 1, total(jnp.where(hit, down(pivot), 0.0)))
        put(at + 2, total(jnp.where(hit, key_down, 0.0)))
        return key_down

    def ends(at, at_count, key_down, first):
        put(at, total(jnp.where(key_down <= lane + first, 1.0, 0.0)) - 1.0)
        put(at_count, total(jnp.where(key_down == lane + first, 1.0, 0.0)))

    local_down = sort(0, lrow[...].astype(jnp.float32), lpiv[...].astype(jnp.float32))
    ends(3, 4, local_down, 0.0)
    owner = cown[...]
    far = ((owner // low) - hi - 1) & (HIGH - 1)
    near = ((owner & (low - 1)) - lo - 1) & (low - 1)
    key = (far * low + near) * rows + crow[...]
    slot_number = lax.broadcasted_iota(jnp.int32, (1, n), 1)
    targets = HIGH * low * rows
    key = jnp.where(slot_number < ccount[0], key, targets)
    cross_down = sort(5, key.astype(jnp.float32), cpiv[...].astype(jnp.float32))
    for p in range(targets // n):
        ends(8 + p, 12 + p, cross_down, float(p * n))


def results_kernel(new_in, adj_in, new_out, adj_out, held, in_sems, out_sems):
    pieces = in_sems.shape[1]
    size = new_in.shape[0] // pieces
    reads, writes = [], []
    for a, (source, target) in enumerate(((new_in, new_out), (adj_in, adj_out))):
        for p in range(pieces):
            span = pl.ds(p * size, size)
            reads.append(
                pltpu.make_async_copy(source.at[span], held.at[a, span], in_sems.at[a, p])
            )
            writes.append(
                pltpu.make_async_copy(held.at[a, span], target.at[span], out_sems.at[a, p])
            )
    for read in reads:
        read.start()
    for read, write in zip(reads, writes):
        read.wait()
        write.start()
    for write in writes:
        write.wait()


def split(x):
    high = x.astype(jnp.bfloat16)
    return high, (x - high.astype(jnp.float32)).astype(jnp.bfloat16)


def three_products(left, right, contract):
    def one(a, b):
        return lax.dot_general(a, b, (contract, ((), ())), preferred_element_type=jnp.float32)

    return one(left[0], right[0]) + (one(left[0], right[1]) + one(left[1], right[0]))


def exchange_kernel(
    low, sections, index, cleft_hbm, cright_hbm, coup_hbm, diag_hbm, seed_hbm, pinv_hbm,
    left_hbm, right_hbm,
    new_hbm, adj_hbm,
    part, got_low, got_high, relayed, later, matrix_high, matrix_low, new, adj,
    base, coup, diag, seed, pinv, cleft, cright, left, right, sums, running,
    load_sem, fs, fr, ls, lr, hs, hr, rs, rr, vs, vr, ns, ads,
):
    rows, width, _ = base.shape
    slots = left.shape[0]
    row = lax.axis_index("row")
    sec = lax.axis_index("section")
    hi, lo = row // low, row % low

    loads = [
        pltpu.make_async_copy(source, target, load_sem.at[i])
        for i, (source, target) in enumerate((
            (pinv_hbm, pinv), (cleft_hbm, cleft), (cright_hbm, cright), (seed_hbm, seed),
            (diag_hbm, diag), (left_hbm, left), (right_hbm, right), (coup_hbm, coup),
        ))
    ]
    for load in loads:
        load.start()
    running[...] = jnp.zeros_like(running)

    @pl.when(hi == 0)
    def _():
        got_high[0] = jnp.zeros(got_high.shape[1:], got_high.dtype)

    @pl.when(hi == HIGH - 1)
    def _():
        got_high[HIGH - 2] = jnp.zeros(got_high.shape[1:], got_high.dtype)


    barrier = pltpu.get_barrier_semaphore()
    for d in range(1, low):
        peer = hi * low + (lo + d) % low
        pl.semaphore_signal(barrier, inc=1, device_id={"row": peer}, device_id_type=MESH)
    for d in range(1, HIGH):
        peer = ((hi + d) % HIGH) * low + lo
        pl.semaphore_signal(barrier, inc=1, device_id={"row": peer}, device_id_type=MESH)

    @pl.when(sec > 0)
    def _():
        pl.semaphore_signal(
            barrier, inc=1, device_id={"section": sec - 1}, device_id_type=MESH
        )

    @pl.when(sec < sections - 1)
    def _():
        pl.semaphore_signal(
            barrier, inc=1, device_id={"section": sec + 1}, device_id_type=MESH
        )

    ends = jnp.where(sec > 0, 1, 0) + jnp.where(sec < sections - 1, 1, 0)
    pl.semaphore_wait(barrier, (low - 1) + (HIGH - 1) + ends)

    own = low - 1
    piece = rows // FIRST_PIECES

    def low_transfer(d, span, far, send_sem, recv_sem):
        return pltpu.make_async_remote_copy(
            src_ref=part.at[d - 1, span, far],
            dst_ref=got_low.at[d - 1, span, far],
            send_sem=send_sem,
            recv_sem=recv_sem,
            device_id={"row": hi * low + (lo + d) % low},
            device_id_type=MESH,
        )

    def first_copy(d, r):
        return low_transfer(d, pl.ds(r * piece, piece), 0, fs.at[d - 1, r], fr.at[d - 1, r])

    def low_copy(d, k):
        return low_transfer(d, k, pl.ds(1, HIGH - 1), ls.at[d - 1, k], lr.at[d - 1, k])

    def high_copy(d, k):
        return pltpu.make_async_remote_copy(
            src_ref=part.at[own, k, d - 1],
            dst_ref=got_high.at[d - 1, k],
            send_sem=hs.at[d - 1, k],
            recv_sem=hr.at[d - 1, k],
            device_id={"row": ((hi + d) % HIGH) * low + lo},
            device_id_type=MESH,
        )

    edge = (hi == 0) | (hi == HIGH - 1)

    def relay_copy(k):
        return pltpu.make_async_remote_copy(
            src_ref=part.at[own, k, jnp.where(hi == 0, HIGH - 2, 0)],
            dst_ref=relayed.at[k],
            send_sem=rs.at[k],
            recv_sem=rr.at[k],
            device_id={"row": jnp.where(hi == 0, 1, HIGH - 2) * low + lo},
            device_id_type=MESH,
        )

    def sends_far(d):
        return {1: hi == HIGH - 1, HIGH - 1: hi == 0}.get(d)

    def gets_none(d):
        return {1: hi == 0, HIGH - 1: hi == HIGH - 1}.get(d)

    def unless(condition, act):
        if condition is None:
            act()
        else:
            pl.when(jnp.logical_not(condition))(act)

    def send_high(d, k):
        unless(sends_far(d), lambda: high_copy(d, k).start())
        if sends_far(d) is not None:
            pl.when(sends_far(d))(lambda: relay_copy(k).start())

    def send_middle(k):
        @pl.when(jnp.logical_not(edge))
        def _():
            relay_copy(k).wait_recv()
            total = part[own, k, 1].astype(jnp.float32) + relayed[k].astype(jnp.float32)
            part[own, k, 1] = total.astype(part.dtype)

        send_high(2, k)

    def merge(k, far):
        total = part[own, k, far].astype(jnp.float32)
        for d in range(1, low):
            total += got_low[d - 1, k, far].astype(jnp.float32)
        part[own, k, far] = total.astype(part.dtype)

    def chain_copy(k, target):
        return pltpu.make_async_remote_copy(
            src_ref=adj.at[k],
            dst_ref=later.at[k],
            send_sem=vs.at[k],
            recv_sem=vr.at[k],
            device_id={"section": target},
            device_id_type=MESH,
        )

    def products(at, pivots, order, first, second, run):
        scaled = [
            jnp.dot(
                first[index[order, j]], pinv[index[pivots, j]],
                preferred_element_type=jnp.float32,
            ).astype(jnp.bfloat16)
            for j in at
        ]
        updates = [
            jnp.dot(half, second[index[order, j]], preferred_element_type=jnp.float32)
            for half, j in zip(scaled, at)
        ]
        for update, j in zip(updates, at):
            same = index[order + 2, j] == index[order + 2, jnp.maximum(j - 1, 0)]
            run = run * jnp.where(same, 1.0, 0.0) + update
            sums[j] = run
        return run

    for load in loads[:3]:
        load.wait()

    def owner_group(q, run):
        far, near = q // low, q % low
        for p in range(CAP // GROUP):
            at = [q * CAP + p * GROUP + i for i in range(GROUP)]
            run = products(at, 6, 5, cleft, cright, run)
        for k in range(rows):
            spot = q * rows + k
            line, place = spot // LANES, spot % LANES
            used = jnp.where(index[12 + line, place] > 0, 1.0, 0.0)
            total = sums[jnp.maximum(index[8 + line, place], 0)] * used
            part[near, k, far] = total.astype(part.dtype)
        for d in range(1, low):

            @pl.when(q == d - 1)
            def _():
                for r in range(FIRST_PIECES):
                    first_copy(d, r).start()

        return run

    def owner_group_and_merge(q, run):
        run = owner_group(q, run)
        r = q - (HIGH * low - FIRST_PIECES)
        for d in range(1, low):
            first_copy(d, r).wait_recv()
        for i in range(piece):
            merge(r * piece + i, 0)
            send_high(1, r * piece + i)
        return run

    plain = HIGH * low - FIRST_PIECES
    run = lax.fori_loop(0, plain, owner_group, jnp.zeros((width, width), jnp.float32))
    lax.fori_loop(plain, HIGH * low, owner_group_and_merge, run)

    for k in range(DEPTH):
        for d in range(1, low):
            low_copy(d, k).start()

    def new_write(k):
        return pltpu.make_async_copy(new.at[k], new_hbm.at[k], ns.at[k])

    def adj_write(k):
        return pltpu.make_async_copy(adj.at[k], adj_hbm.at[k], ads.at[k])

    def local_group(g, run):
        at = [g * GROUP + i for i in range(GROUP)]
        return products(at, 1, 0, left, right, run)

    def local_row(k, carry):
        used = jnp.where(index[4, k] > 0, 1.0, 0.0)
        total = sums[jnp.maximum(index[3, k], 0)] * used
        base[k] = coup[k].astype(jnp.float32) - total
        return carry

    def finish_row(j, carry):
        for d in range(1, HIGH):
            unless(gets_none(d), lambda d=d: high_copy(d, j).wait_recv())
        total = part[own, j, HIGH - 1].astype(jnp.float32)
        for d in range(1, HIGH):
            total += got_high[d - 1, j].astype(jnp.float32)
        total = base[j] - total
        new[j] = total
        new_write(j).start()
        matrix_high[j], matrix_low[j] = split(
            three_products(split(diag[j]), split(total), ((1,), (0,)))
        )
        return carry

    def solve_row(m, carry):
        chain_copy(m, sec).wait_recv()
        adj[m] -= three_products(
            split(later[m]), (matrix_high[m], matrix_low[m]), ((1,), (1,))
        )

        @pl.when(sec > 0)
        def _():
            chain_copy(m, sec - 1).start()

        adj_write(m).start()
        return carry

    def finished(c):
        done = jnp.where(c < rows, jnp.clip(c - LAG + 1, 0, rows), rows)
        return jnp.where(c < LOCAL_STEPS, 0, done)


    def step(c, carry):
        @pl.when(c + DEPTH < rows)
        def _():
            for d in range(1, low):
                low_copy(d, c + DEPTH).start()

        @pl.when(c < rows)
        def _():
            for d in range(1, low):
                low_copy(d, c).wait_recv()
            for far in range(1, HIGH):
                merge(c, far)
                if far == HIGH - 2:
                    send_high(HIGH - 1, c)

        @pl.when((c >= 1) & (c <= rows))
        def _():
            send_middle(c - 1)

        @pl.when(c == 0)
        def _():
            for load in loads[3:]:
                load.wait()

        @pl.when(c < rows)
        def _():
            adj[c] = three_products(split(seed[c]), split(diag[c]), ((1,), (1,)))

        @pl.when((c < rows) & (sec == sections - 1))
        def _():
            chain_copy(c, sec - 1).start()
            adj_write(c).start()

        @pl.when(c < LOCAL_STEPS)
        def _():
            per_step = slots // (LOCAL_STEPS * GROUP)
            running[...] = lax.fori_loop(
                c * per_step, (c + 1) * per_step, local_group, running[...]
            )

        @pl.when(c == LOCAL_STEPS - 1)
        def _():
            lax.fori_loop(0, rows, local_row, 0)

        lax.fori_loop(finished(c - 1), finished(c), finish_row, 0)
        delay = sections - 2 - sec

        @pl.when(sec < sections - 1)
        def _():
            lax.fori_loop(finished(c - 1 - delay), finished(c - delay), solve_row, 0)

        return carry

    lax.fori_loop(0, rows + sections - 1, step, 0)

    def drain(k, carry):
        new_write(k).wait()
        adj_write(k).wait()
        for d in range(1, low):
            low_copy(d, k).wait_send()
        for d in range(1, HIGH):
            unless(sends_far(d), lambda d=d: high_copy(d, k).wait_send())

        @pl.when(edge)
        def _():
            relay_copy(k).wait_send()

        @pl.when(sec > 0)
        def _():
            chain_copy(k, sec - 1).wait_send()

        return carry

    lax.fori_loop(0, rows, drain, 0)
    for r in range(FIRST_PIECES):
        for d in range(1, low):
            first_copy(d, r).wait_send()


def per_device(
    coupling,
    diag_inverse,
    pivot_inverse,
    cross_left,
    cross_right,
    cross_pivot,
    cross_owner,
    foreign_target_row,
    cross_count,
    local_left,
    local_right,
    local_pivot,
    local_target,
    adjoint_seed,
):
    rows, width, _ = coupling.shape
    groups = lax.axis_size("row")
    sections = lax.axis_size("section")
    low = groups // HIGH
    slots, local_slots = cross_left.shape[0], local_left.shape[0]
    block = (width, width)
    scalars = pl.BlockSpec(memory_space=pltpu.SMEM)
    vector = pl.BlockSpec(memory_space=pltpu.VMEM)

    def flat(x):
        return x.reshape(1, x.size)

    index = pl.pallas_call(
        functools.partial(order_kernel, low, rows),
        out_shape=jax.ShapeDtypeStruct((16, slots), jnp.int32),
        in_specs=[scalars] + [vector] * 5,
        out_specs=vector,
        name="order",
    )(cross_count, flat(cross_pivot), flat(cross_owner), flat(foreign_target_row),
      flat(local_pivot), flat(local_target))

    hbm = pl.BlockSpec(memory_space=pl.ANY)
    dma = pltpu.SemaphoreType.DMA
    outs = (
        jax.ShapeDtypeStruct((rows,) + block, jnp.float32),
        jax.ShapeDtypeStruct((rows,) + block, jnp.float32),
    )
    results = pl.pallas_call(
        functools.partial(exchange_kernel, low, sections),
        out_shape=outs,
        in_specs=[scalars] + [hbm] * 8,
        out_specs=(hbm, hbm),
        scratch_shapes=[
            pltpu.VMEM((low, rows, HIGH) + block, jnp.bfloat16),
            pltpu.VMEM((low - 1, rows, HIGH) + block, jnp.bfloat16),
            pltpu.VMEM((HIGH - 1, rows) + block, jnp.bfloat16),
            pltpu.VMEM((rows,) + block, jnp.bfloat16),
            pltpu.VMEM((rows,) + block, jnp.float32),
            pltpu.VMEM((rows,) + block, jnp.bfloat16),
            pltpu.VMEM((rows,) + block, jnp.bfloat16),
            pltpu.VMEM((rows,) + block, jnp.float32),
            pltpu.VMEM((rows,) + block, jnp.float32),
            pltpu.VMEM((rows,) + block, jnp.float32),
            pltpu.VMEM(coupling.shape, coupling.dtype),
            pltpu.VMEM(diag_inverse.shape, jnp.float32),
            pltpu.VMEM(adjoint_seed.shape, jnp.float32),
            pltpu.VMEM(pivot_inverse.shape, pivot_inverse.dtype),
            pltpu.VMEM(cross_left.shape, cross_left.dtype),
            pltpu.VMEM(cross_right.shape, cross_right.dtype),
            pltpu.VMEM(local_left.shape, local_left.dtype),
            pltpu.VMEM(local_right.shape, local_right.dtype),
            pltpu.VMEM((local_slots,) + block, jnp.float32),
            pltpu.VMEM(block, jnp.float32),
            dma((8,)),
            dma((low - 1, FIRST_PIECES)),
            dma((low - 1, FIRST_PIECES)),
            dma((low - 1, rows)),
            dma((low - 1, rows)),
            dma((HIGH - 1, rows)),
            dma((HIGH - 1, rows)),
            dma((rows,)),
            dma((rows,)),
            dma((rows,)),
            dma((rows,)),
            dma((rows,)),
            dma((rows,)),
        ],
        compiler_params=pltpu.CompilerParams(
            collective_id=0, has_side_effects=True, vmem_limit_bytes=VMEM_LIMIT
        ),
        name="exchange",
    )(index, cross_left, cross_right, coupling, diag_inverse, adjoint_seed, pivot_inverse,
      local_left, local_right)
    return pl.pallas_call(
        results_kernel,
        out_shape=outs,
        in_specs=[hbm, hbm],
        out_specs=(hbm, hbm),
        scratch_shapes=[pltpu.VMEM((2, rows) + block, jnp.float32), dma((2, 4)), dma((2, 4))],
        compiler_params=pltpu.CompilerParams(vmem_limit_bytes=VMEM_LIMIT),
        name="results",
    )(*results)


def solution(mesh):
    spread = P(("section", "row"))
    return jax.shard_map(
        per_device,
        mesh=mesh,
        in_specs=(spread,) * 14,
        out_specs=(spread, spread),
        check_vma=False,
    )
```
